128 devices in a mesh: gr: 16 (over y_lo, z, core), gc: 8 (over x, y_hi).
Axes of the slice: x: 4, y: 4 (y_hi: 2, y_lo: 2; y = y_hi * 2 + y_lo), z: 4, core: 2. Of those that a mesh axis runs over, the one named last changes fastest.
Arguments:
- features: bfloat16 [65536, 256], P(('gr', 'gc')), may hold values from -6 to 6
- block_values: bfloat16 [16, 8, 384, 128, 128], P('gr', 'gc')
- block_row: int32 [16, 8, 384], P('gr', 'gc'), may hold values from 0 to 31
- block_col: int32 [16, 8, 384], P('gr', 'gc'), may hold values from 0 to 63
- block_count: int32 [16, 8], P('gr', 'gc'), may hold values from 96 to 384, as said below
- weight_self: bfloat16 [256, 256], replicated, may hold values from -0.375 to 0.375
- weight_neigh: bfloat16 [256, 256], replicated, may hold values from -0.375 to 0.375
- bias: float32 [256], replicated, may hold values from -0.5 to 0.5
- cotangent: bfloat16 [65536, 256], P(('gr', 'gc')), may hold values from -6 to 6
Outputs:
- activations: bfloat16 [65536, 256], P(('gr', 'gc'))
- grad_features: bfloat16 [65536, 256], P(('gr', 'gc'))
- grad_self: float32 [256, 256], replicated
- grad_neigh: float32 [256, 256], replicated
- grad_bias: float32 [256], replicated
The draws below stay inside these ranges and needn't reach their ends.
Inputs may be any that keep to these rules, and one draw needn't show every extreme that they name: Slots 0 to block_count - 1 of a grid cell are live; some grid cell holds exactly 384 live slots.
All inputs are finite; a program needn't handle non-finite values.
Results may differ from the reference program's by a relative error of at most 0.007.
Values may be sent and summed in bfloat16 or wider, within the bound.
A program may use at most 128 MiB of HBM per device.

```python
import math
import jax
import jax.numpy as jnp
from jax import lax

D = 256
ROWS_DEV = 512
NB = 384
NODES = 65536
BLOCK_ROWS = 32
BLOCK_COLS = 64
N_GR = 16
N_GC = 8


def draw_block_count(key, part):
    key = jax.random.fold_in(key, 11)
    first, second = jax.random.split(key)
    lowest = max(1, NB // 4)
    cells = N_GR * N_GC
    counts = jax.random.randint(first, (cells,), lowest, NB + 1)
    fullest = jax.random.randint(second, (), 0, cells)
    counts = jnp.where(jnp.arange(cells) == fullest, NB, counts)
    return counts.reshape(N_GR, N_GC).astype(jnp.int32)


def draw_block_values(key, part):
    key = jax.random.fold_in(key, 5)
    first, second = jax.random.split(key)
    shape = (N_GR, N_GC, NB, 128, 128)
    present = jax.random.randint(second, shape, 0, 64) == 0
    values = jnp.clip(2.0 * jax.random.normal(first, shape, jnp.float32), -8.0, 8.0)
    return jnp.where(present, values, 0.0).astype(jnp.bfloat16)


def touch_ends(values, rng, low, high):
    longest = values.shape.index(max(values.shape))
    spots = []
    for shift in (0, 1):
        where = [jax.random.randint(jax.random.fold_in(rng, axis), (), 0, length) for axis, length in enumerate(values.shape)]
        where[longest] = (where[longest] + shift) % values.shape[longest]
        spots.append(tuple(where))
    return values.at[spots[0]].set(low).at[spots[1]].set(high)


def levels(own_key, shape, pieces, least, high):
    gain, own = 1.0, jax.random.fold_in(own_key, 6)
    for axis_at, blocks in pieces:
        draws = jnp.exp(jax.random.uniform(jax.random.fold_in(own, axis_at), (blocks,), jnp.float32, least / len(pieces), high / len(pieces)))
        gain = gain * jnp.repeat(draws, shape[axis_at] // blocks).reshape([-1 if axis == axis_at else 1 for axis in range(len(shape))])
    return gain


def scatter_about(rng, shape, deviation, most, pieces=(), kind=jnp.bfloat16):
    drawn = jax.random.normal(rng, shape, jnp.float32) * deviation
    if len(pieces) > 0:
        drawn = levels(rng, shape, pieces, -0.22, 0.18) * drawn
    return jnp.clip(drawn, min=-most, max=most).astype(kind)


def setup_inputs(seed: int = 0) -> dict:
    seeds = jax.random.split(jax.random.key(seed), 10)
    return {
        "features": scatter_about(seeds[0], (NODES, D), 1.0, 6.0, ((0, 128),)),
        "block_values": draw_block_values(jax.random.fold_in(seeds[9], 71), 0),
        "block_row": touch_ends(jax.random.randint(seeds[2], (N_GR, N_GC, NB), 0, BLOCK_ROWS), jax.random.fold_in(seeds[2], 1), 0, BLOCK_ROWS - 1).astype(jnp.int32),
        "block_col": touch_ends(jax.random.randint(seeds[3], (N_GR, N_GC, NB), 0, BLOCK_COLS), jax.random.fold_in(seeds[3], 1), 0, BLOCK_COLS - 1).astype(jnp.int32),
        "block_count": draw_block_count(jax.random.fold_in(seeds[9], 71), 0),
        "weight_self": scatter_about(seeds[5], (D, D), D ** -0.5, 0.375),
        "weight_neigh": scatter_about(seeds[6], (D, D), D ** -0.5, 0.375),
        "bias": jnp.clip(jax.random.uniform(seeds[7], (D,), jnp.float32, -0.5, 0.5), -0.5, 0.5),
        "cotangent": scatter_about(seeds[8], (NODES, D), 1.0, 6.0, ((0, 128),)),
    }


def tile_starts(block_row, block_col):
    grid_row = jnp.arange(N_GR, dtype=jnp.int32)[:, None, None]
    grid_col = jnp.arange(N_GC, dtype=jnp.int32)[None, :, None]
    row_start = (grid_row * BLOCK_ROWS + block_row) * 128
    local = block_col * 128
    col_start = (local // ROWS_DEV * N_GC + grid_col) * ROWS_DEV + local % ROWS_DEV
    return (row_start.reshape(-1, NB).astype(jnp.int32), col_start.reshape(-1, NB).astype(jnp.int32))

def sparse_apply(tiles, live, take_start, put_start, source, transpose):
    offsets = jnp.arange(128, dtype=jnp.int32)
    width = source.shape[1]

    def step(total, item):
        tile, keep, take, put = item
        picked = source[take[:, None] + offsets[None, :]].astype(jnp.float32)
        form = 'bji,bjf->bif' if transpose else 'bij,bjf->bif'
        prods = jnp.einsum(form, tile.astype(jnp.float32), picked) * keep[:, None, None]
        where = (put[:, None] + offsets[None, :]).reshape(-1)
        return (total.at[where].add(prods.reshape(-1, width)), None)
    total = jnp.zeros((source.shape[0], width), jnp.float32)
    total, _ = lax.scan(step, total, (tiles, live, take_start, put_start))
    return total

def row_degrees(tiles, live, put_start):
    offsets = jnp.arange(128, dtype=jnp.int32)

    def step(total, item):
        tile, keep, put = item
        nonzero = lax.optimization_barrier(jnp.sum((tile != 0).astype(jnp.float32), axis=2)) * keep[:, None]
        where = (put[:, None] + offsets[None, :]).reshape(-1)
        return (total.at[where].add(nonzero.reshape(-1)), None)
    total = jnp.zeros((NODES,), jnp.float32)
    total, _ = lax.scan(step, total, (tiles, live, put_start))
    return jnp.maximum(total, 1.0)

def reference(features, block_values, block_row, block_col, block_count, weight_self, weight_neigh, bias, cotangent):
    row_start, col_start = tile_starts(block_row, block_col)
    tiles = block_values.reshape(-1, NB, 128, 128)
    slots = jnp.arange(NB, dtype=jnp.int32)[None, :]
    live = (slots < block_count.reshape(-1, 1)).astype(jnp.float32)
    counts = row_degrees(tiles, live, row_start)[:, None]
    summed = sparse_apply(tiles, live, col_start, row_start, features, False)
    neigh_mean = (summed / counts).astype(jnp.bfloat16)
    preact = jnp.dot(features, weight_self, preferred_element_type=jnp.float32) + jnp.dot(neigh_mean, weight_neigh, preferred_element_type=jnp.float32) + bias[None, :]
    sigma = jax.nn.sigmoid(preact)
    activations = (preact * sigma).astype(jnp.bfloat16)
    grad_pre = (cotangent.astype(jnp.float32) * sigma * (1.0 + preact * (1.0 - sigma))).astype(jnp.bfloat16)
    back_rows = (jnp.dot(grad_pre, weight_neigh.T, preferred_element_type=jnp.float32) / counts).astype(jnp.bfloat16)
    back_sum = sparse_apply(tiles, live, row_start, col_start, back_rows, True)
    grad_features = (jnp.dot(grad_pre, weight_self.T, preferred_element_type=jnp.float32) + back_sum).astype(jnp.bfloat16)
    scale = 1.0 / math.sqrt(NODES)
    grad_self = jnp.dot(features.T, grad_pre, preferred_element_type=jnp.float32) * scale
    grad_neigh = jnp.dot(neigh_mean.T, grad_pre, preferred_element_type=jnp.float32) * scale
    grad_bias = lax.optimization_barrier(jnp.sum(grad_pre.astype(jnp.float32), axis=0)) * scale
    return (activations, grad_features, grad_self, grad_neigh, grad_bias)
```

```python
import functools

import jax
import jax.numpy as jnp
from jax import lax
from jax.experimental import pallas as pl
from jax.experimental.pallas import tpu as pltpu
from jax.sharding import PartitionSpec as P

MESH = pl.DeviceIdType.MESH
VMEM = pltpu.VMEM
SMEM = pltpu.SMEM

SLOTS = 384
ROW_BLOCKS = 32
COL_BLOCKS = 64
FWD_PAIRS = 208
BWD_PAIRS = 224
UNROLL = 16
SPLIT_ROWS = 208
SEMS = 128
bf16, f32, i32 = jnp.bfloat16, jnp.float32, jnp.int32


def order_slots(key_lane, key_sub, other_sub, count, keys, empty):
    lane = lax.broadcasted_iota(i32, (1, SLOTS), 1)
    sub = lax.broadcasted_iota(i32, (SLOTS, 1), 0)
    key_l = jnp.where(lane < count, key_lane, -1)
    key_s = jnp.where(sub < count, key_sub, -2)
    before = (key_s == key_l) & (lane < sub)
    rank = jnp.sum(jnp.where(before, 1.0, 0.0), axis=1, keepdims=True)
    k_lane = lax.broadcasted_iota(i32, (1, 128), 1)
    k_sub = lax.broadcasted_iota(i32, (keys, 1), 0)
    in_lane = jnp.sum(jnp.where(key_s == k_lane, 1.0, 0.0), axis=0, keepdims=True)
    in_sub = jnp.sum(jnp.where(key_l == k_sub, 1.0, 0.0), axis=1, keepdims=True)
    pairs_l = jnp.floor((in_lane + 1.0) * 0.5)
    pairs_s = jnp.floor((in_sub + 1.0) * 0.5)
    begin = jnp.sum(jnp.where(k_lane < key_s, pairs_l, 0.0), axis=1, keepdims=True)
    place = jnp.where(sub < count, 2.0 * begin + rank, -1.0)
    begin_s = jnp.sum(jnp.where(k_lane < k_sub, pairs_l, 0.0), axis=1, keepdims=True)
    begin_l = jnp.sum(jnp.where(k_sub < k_lane, pairs_s, 0.0), axis=0, keepdims=True)
    spot = lax.broadcasted_iota(i32, (1, 512), 1).astype(f32)
    here = place == spot
    slot = SLOTS - jnp.sum(jnp.where(here, (SLOTS - sub).astype(f32), 0.0), axis=0, keepdims=True)
    other = jnp.sum(jnp.where(here, other_sub.astype(f32), 0.0), axis=0, keepdims=True)
    first = (begin_s == spot) & (pairs_s > 0.0)
    keep = 1.0 - jnp.sum(jnp.where(first, 1.0, 0.0), axis=0, keepdims=True)
    last = jnp.where(pairs_l > 0.0, begin_l + pairs_l - 1.0, float(empty))
    last = jnp.concatenate([last] * 4, axis=1)
    return jnp.concatenate([slot, other, keep, last], axis=0).astype(i32)


def plan_kernel(count_ref, row_l, col_l, row_s, col_s, out_ref):
    count = count_ref[0, 0]
    out_ref[0:4, :] = order_slots(row_l[...], row_s[...], col_s[...], count, ROW_BLOCKS, FWD_PAIRS)
    out_ref[4:8, :] = order_slots(col_l[...], col_s[...], row_s[...], count, COL_BLOCKS, BWD_PAIRS)


def plan(block_row, block_col, block_count):
    return pl.pallas_call(
        plan_kernel,
        out_shape=jax.ShapeDtypeStruct((8, 512), i32),
        in_specs=[pl.BlockSpec(memory_space=SMEM)] + [pl.BlockSpec(memory_space=VMEM)] * 4,
        out_specs=pl.BlockSpec(memory_space=VMEM),
        name="plan",
    )(
        block_count.reshape(1, 1),
        block_row.reshape(1, SLOTS),
        block_col.reshape(1, SLOTS),
        block_row.reshape(SLOTS, 1),
        block_col.reshape(SLOTS, 1),
    )


class Net:
    def __init__(self, send, recv):
        self.send, self.recv, self.started = send, recv, []

    def put(self, src, dst, device):
        at = len(self.started)
        copy = pltpu.make_async_remote_copy(
            src_ref=src,
            dst_ref=dst,
            send_sem=self.send.at[at],
            recv_sem=self.recv.at[at],
            device_id=device,
            device_id_type=MESH,
        )
        copy.start()
        self.started.append(copy)
        return copy

    def finish(self):
        for copy in self.started:
            copy.wait_send()


def layer_kernel(
    meta,
    feats,
    tiles_hbm,
    w_self_hbm,
    w_neigh_hbm,
    bias_ref,
    cot_hbm,
    act_out,
    gfeat_out,
    gself_out,
    gneigh_out,
    gbias_out,
    tiles,
    xg,
    prods,
    acc,
    degp,
    degs,
    degr,
    rowsum,
    bg,
    csend,
    crecv,
    csum,
    fwd_bufs,
    bwd_bufs,
    total,
    own_part,
    w_self,
    w_neigh,
    cot,
    neigh,
    grad_pre,
    wg,
    w1,
    w2,
    w3,
    w4,
    bias0,
    bias_s,
    rs_,
    rx_,
    rz_,
    rp_,
    rh_,
    rb_,
    wfull,
    send_sem,
    recv_sem,
    local_sem,
):
    gr, gc = lax.axis_index("gr"), lax.axis_index("gc")
    a, z, core = gr // 8, (gr // 2) % 4, gr % 2
    x, h = gc // 2, gc % 2

    def device(a_=None, z_=None, core_=None, x_=None, h_=None):
        a_ = a if a_ is None else a_
        z_ = z if z_ is None else z_
        core_ = core if core_ is None else core_
        x_ = x if x_ is None else x_
        h_ = h if h_ is None else h_
        return (a_ * 8 + z_ * 2 + core_, x_ * 2 + h_)

    sib = device(core_=1 - core)
    z_peer = {d: device(z_=(z + d) % 4) for d in (1, 2, 3)}
    x_peer = {d: device(x_=(x + d) % 4) for d in (1, 2, 3)}
    a_peer = device(a_=1 - a)
    h_peer = device(h_=1 - h)
    diagonal = {d: device(x_=(x + d) % 4, h_=1 - h) for d in (1, 2, 3)}

    loads = [
        pltpu.make_async_copy(tiles_hbm, tiles.at[pl.ds(0, SLOTS)], local_sem.at[0]),
        pltpu.make_async_copy(feats, xg.at[pl.ds(4 * gr, 4)], local_sem.at[1]),
        pltpu.make_async_copy(w_self_hbm, w_self, local_sem.at[2]),
        pltpu.make_async_copy(w_neigh_hbm, w_neigh, local_sem.at[3]),
        pltpu.make_async_copy(cot_hbm, cot, local_sem.at[4]),
    ]
    for copy in loads:
        copy.start()

    barrier = pltpu.get_barrier_semaphore()
    peers = [sib, a_peer, h_peer]
    peers += list(z_peer.values()) + list(x_peer.values()) + list(diagonal.values())
    for peer in peers:
        pl.semaphore_signal(barrier, inc=1, device_id=peer, device_id_type=MESH)
    pl.semaphore_wait(barrier, len(peers))
    net = Net(send_sem, recv_sem)

    def gather(buf, base, ring, side, up, down, across, own, forward, steps):
        def piece(d, other, j):
            return buf.at[pl.ds(base((ring + d) % 4, (1 - side) if other else side) + 2 * j, 2)]

        def push(d, other, j, device_id):
            return net.put(piece(d, other, j), piece(d, other, j), device_id)

        first = {0: {}, 1: {}}
        targets = (up, down, across)
        for j, way in ((0, 0), (1, 1), (1, 2), (0, 2), (1, 0), (0, 1)):
            first[j][way] = net.put(own(j), piece(0, 0, j), targets[way])
        own_sib = forward(0, 0, None)

        first[0][0].wait_recv()
        up_1 = push(3, 0, 0, up)
        across_0 = push(3, 0, 0, across)
        sent = [forward(3, 0, 0)]
        first[1][1].wait_recv()
        down_1 = push(1, 0, 1, down)
        across_1 = push(1, 0, 1, across)
        sent.append(forward(1, 0, 1))
        first[1][2].wait_recv()
        up_2 = push(0, 1, 1, up)
        sent.append(forward(0, 1, 1))
        first[0][2].wait_recv()
        down_2 = push(0, 1, 0, down)
        sent.append(forward(0, 1, 0))
        first[1][0].wait_recv()
        sent.append(forward(3, 0, 1))
        first[0][1].wait_recv()
        sent.append(forward(1, 0, 0))
        steps[0]()
        across_0.wait_recv()
        up_3 = push(3, 1, 0, up)
        sent.append(forward(3, 1, 0))
        across_1.wait_recv()
        down_3 = push(1, 1, 1, down)
        sent.append(forward(1, 1, 1))
        up_1.wait_recv()
        sent.append(forward(2, 0, 0))
        down_1.wait_recv()
        sent.append(forward(2, 0, 1))
        steps[1]()
        up_2.wait_recv()
        sent.append(forward(3, 1, 1))
        down_2.wait_recv()
        sent.append(forward(1, 1, 0))
        up_3.wait_recv()
        sent.append(forward(2, 1, 0))
        down_3.wait_recv()
        sent.append(forward(2, 1, 1))
        for copy in [own_sib] + sent:
            if copy is not None:
                copy.wait_recv()

    def scatter(bufs, src, at, ring, side, ring_peer, across, ready, steps):
        ra_buf, rb_buf, r2a_src, r2a_buf, r2b_src, r2b_buf = bufs
        top, low = pl.ds(0, SPLIT_ROWS), pl.ds(SPLIT_ROWS, 512 - SPLIT_ROWS)
        near, far, far_b = {}, {}, {}
        for d in (2, 1, 3, 0):
            ready(d, 1)
            far_b[d] = net.put(src.at[at(d, 1), low], rb_buf.at[d], across)
            if d:
                far[d] = net.put(src.at[at(d, 1), top], ra_buf.at[2 * d - 2], ring_peer[d])
        for d in (2, 1, 3, 0):
            ready(d, 0)
            if d:
                near[d] = net.put(src.at[at(d, 0), top], ra_buf.at[2 * d - 1], ring_peer[d])
        steps[0]()
        second = {}
        for d in (2, 1, 3):
            far_b[d].wait_recv()
            part = src[at(d, 0), low].astype(f32) + rb_buf[d].astype(f32)
            r2b_src[d - 1] = part.astype(bf16)
            second[d] = net.put(r2b_src.at[d - 1], r2b_buf.at[d - 1], ring_peer[d])
        part = src[at(0, 1), top].astype(f32)
        for d in (1, 3, 2):
            far[d].wait_recv()
            part += ra_buf[2 * d - 2].astype(f32)
        r2a_src[...] = part.astype(bf16)
        second_a = net.put(r2a_src, r2a_buf, across)
        part = src[at(0, 0), top].astype(f32)
        for d in (1, 3, 2):
            near[d].wait_recv()
            part += ra_buf[2 * d - 1].astype(f32)
        steps[1]()
        second_a.wait_recv()
        total[top, :] = part + r2a_buf[...].astype(f32)
        far_b[0].wait_recv()
        part = src[at(0, 0), low].astype(f32) + rb_buf[0].astype(f32)
        for d in (1, 3, 2):
            second[d].wait_recv()
            part += r2b_buf[d - 1].astype(f32)
        total[low, :] = part

    def multiply(base, source, backward, pairs):
        acc[...] = jnp.zeros_like(acc)
        prods[pairs] = jnp.zeros((128, 256), bf16)

        def body(step, carry):
            for u in range(UNROLL):
                p = step * UNROLL + u
                left = [tiles[meta[base, 2 * p + i]] for i in (0, 1)]
                right = jnp.concatenate([source[meta[base + 1, 2 * p + i]] for i in (0, 1)], axis=0)
                if backward:
                    left = jnp.concatenate(left, axis=0)
                    form = (((0,), (0,)), ((), ()))
                else:
                    left = jnp.concatenate(left, axis=1)
                    form = (((1,), (0,)), ((), ()))
                product = lax.dot_general(left, right, form, preferred_element_type=f32)
                running = product + jnp.where(meta[base + 2, p] != 0, acc[...], 0.0)
                acc[...] = running
                prods[p] = running.astype(bf16)
            return carry

        lax.fori_loop(0, pairs // UNROLL, body, 0)

    def count_some(begin, end):
        ones = jnp.ones((8, 256), bf16)

        def body(step, carry):
            for u in range(UNROLL):
                p = step * UNROLL + u
                pair = jnp.concatenate([tiles[meta[0, 2 * p + i]] for i in (0, 1)], axis=1)
                present = jnp.where(pair != 0, jnp.ones((), bf16), jnp.zeros((), bf16))
                found = lax.dot_general(
                    ones, present, (((1,), (1,)), ((), ())), preferred_element_type=f32
                )
                running = found + jnp.where(meta[2, p] != 0, degp[FWD_PAIRS], 0.0)
                degp[FWD_PAIRS] = running
                degp[p] = running
            return carry

        lax.fori_loop(begin, end, body, 0)

    def count_first():
        loads[0].wait()
        tiles[SLOTS] = jnp.zeros((128, 128), bf16)
        degp[FWD_PAIRS] = jnp.zeros((8, 128), f32)
        count_some(0, 7)

    degree_copies = []

    def count_last():
        count_some(7, 13)
        degp[FWD_PAIRS] = jnp.zeros((8, 128), f32)
        sub = lax.broadcasted_iota(i32, (8, 128), 0)
        for g in range(8):
            rows = jnp.zeros((8, 128), f32)
            for j in range(4):
                rows = jnp.where(sub == j, degp[meta[3, 4 * g + j]], rows)
            degs[g] = rows
        for d in range(4):
            for e in (0, 1):
                if (d, e) == (0, 0):
                    continue
                target = h_peer if d == 0 else (diagonal[d] if e else x_peer[d])
                index = ((x + d) % 4) * 2 + ((1 - h) if e else h)
                degree_copies.append(net.put(degs.at[index], degr.at[2 * d + e], target))
        for copy in loads[1:]:
            copy.wait()
        for j in range(4):
            own_part[pl.ds(128 * j, 128), :] = (
                jnp.dot(xg[4 * gr + j], w_self[...], preferred_element_type=f32) + bias_ref[...]
            )

    def to_sibling(d, other, j):
        if j is None:
            own = xg.at[pl.ds(4 * gr, 4)]
            return net.put(feats, own, sib)
        at = 4 * ((1 - a if other else a) * 8 + ((z + d) % 4) * 2 + core) + 2 * j
        return net.put(xg.at[pl.ds(at, 2)], xg.at[pl.ds(at, 2)], sib)

    gather(
        xg,
        lambda ring, side: 4 * (side * 8 + ring * 2 + core),
        z,
        a,
        z_peer[1],
        z_peer[3],
        a_peer,
        lambda j: feats.at[pl.ds(2 * j, 2)],
        to_sibling,
        (count_first, count_last),
    )

    multiply(0, xg, False, FWD_PAIRS)

    def rows_at(d, other):
        return ((x + d) % 4) * 2 + ((1 - h) if other else h)

    def rows_ready(d, other):
        shard = rows_at(d, other)
        for j in range(4):
            rowsum[shard, pl.ds(128 * j, 128), :] = prods[meta[3, 4 * shard + j]]

    def nothing():
        pass

    scatter(fwd_bufs, rowsum, rows_at, x, h, x_peer, h_peer, rows_ready, (nothing, nothing))

    degree = degs[gc]
    for copy in degree_copies:
        copy.wait_recv()
    for slot in range(1, 8):
        degree += degr[slot]
    degree = jnp.maximum(degree, 1.0)
    gathered = {}
    for j in range(4):
        rows = pl.ds(128 * j, 128)
        counts = jnp.broadcast_to(degree[j : j + 1, :], (128, 128)).T
        counts = jnp.concatenate([counts, counts], axis=1)
        mean = (total[rows, :] / counts).astype(bf16)
        neigh[rows, :] = mean
        preact = own_part[rows, :] + jnp.dot(mean, w_neigh[...], preferred_element_type=f32)
        sigma = jax.nn.sigmoid(preact)
        act_out[rows, :] = (preact * sigma).astype(bf16)
        grad = cot[rows, :].astype(f32) * sigma * (1.0 + preact * (1.0 - sigma))
        grad = grad.astype(bf16)
        grad_pre[rows, :] = grad
        projected = lax.dot_general(
            grad, w_neigh[...], (((1,), (1,)), ((), ())), preferred_element_type=f32
        )
        bg[4 * gc + j] = (projected / counts).astype(bf16)

    contract_rows = (((0,), (0,)), ((), ()))
    state = {}

    def weight_grads():
        own = jnp.concatenate([xg[4 * gr + j] for j in range(4)], axis=0)
        grad = grad_pre[...]
        wg[0:256, :] = lax.dot_general(own, grad, contract_rows, preferred_element_type=f32)
        wg[256:512, :] = lax.dot_general(
            neigh[...], grad, contract_rows, preferred_element_type=f32
        )
        bias0[...] = jnp.broadcast_to(
            jnp.sum(grad.astype(f32), axis=0, keepdims=True), (8, 256)
        )
        state["s"] = [
            net.put(wg.at[pl.ds((1 - core) * 256, 256)], rs_, sib),
            net.put(bias0, rb_.at[0], sib),
        ]
        own_part[...] = lax.dot_general(
            grad, w_self[...], (((1,), (1,)), ((), ())), preferred_element_type=f32
        )

    def sum_sib():
        for copy in state["s"]:
            copy.wait_recv()
        w1[...] = wg[pl.ds(core * 256, 256), :] + rs_[...]
        bias_s[0] = bias0[...] + rb_[0]
        state["x"] = []
        for d in (2, 1, 3):
            src = w1.at[pl.ds(((x + d) % 4) * 64, 64)]
            state["x"].append(net.put(src, rx_.at[d - 1], x_peer[d]))
            state["x"].append(net.put(bias_s.at[0], rb_.at[d], x_peer[d]))

    def sum_x():
        for copy in state["x"]:
            copy.wait_recv()
        w2[...] = w1[pl.ds(x * 64, 64), :] + rx_[0] + rx_[1] + rx_[2]
        bias_s[1] = bias_s[0] + rb_[1] + rb_[2] + rb_[3]
        state["z"] = []
        for d in (2, 1, 3):
            src = w2.at[pl.ds(((z + d) % 4) * 16, 16)]
            state["z"].append(net.put(src, rz_.at[d - 1], z_peer[d]))
            state["z"].append(net.put(bias_s.at[1], rb_.at[3 + d], z_peer[d]))

    def sum_z():
        for copy in state["z"]:
            copy.wait_recv()
        w3[...] = w2[pl.ds(z * 16, 16), :] + rz_[0] + rz_[1] + rz_[2]
        bias_s[2] = bias_s[1] + rb_[4] + rb_[5] + rb_[6]
        state["p"] = [
            net.put(w3.at[pl.ds((1 - a) * 8, 8)], rp_, a_peer),
            net.put(bias_s.at[2], rb_.at[7], a_peer),
        ]

    def sum_p():
        for copy in state["p"]:
            copy.wait_recv()
        w4[...] = w3[pl.ds(a * 8, 8), :] + rp_[...]
        bias_s[3] = bias_s[2] + rb_[7]
        state["h"] = [net.put(w4, rh_, h_peer), net.put(bias_s.at[3], rb_.at[8], h_peer)]

    def share(rows, size, targets):
        part = wfull.at[pl.ds(rows, size)]
        return [net.put(part, part, target) for target in targets]

    def sum_h():
        for copy in state["h"]:
            copy.wait_recv()
        wfull[pl.ds(core * 256 + x * 64 + z * 16 + a * 8, 8), :] = w4[...] + rh_[...]
        gbias_out[...] = (bias_s[3] + rb_[8])[0:1, :] * (1.0 / 256.0)
        state["gp"] = share(core * 256 + x * 64 + z * 16 + a * 8, 8, [a_peer])

    def share_z():
        for copy in state["gp"]:
            copy.wait_recv()
        state["gz"] = share(core * 256 + x * 64 + z * 16, 16, list(z_peer.values()))

    def share_x():
        for copy in state["gz"]:
            copy.wait_recv()
        state["gx"] = share(core * 256 + x * 64, 64, list(x_peer.values()))

    def share_sib():
        for copy in state["gx"]:
            copy.wait_recv()
        state["gs"] = share(core * 256, 256, [sib])

    def mid_gather():
        sum_sib()

    def late_gather():
        sum_x()

    def no_forward(d, other, j):
        if j is None:
            weight_grads()
        return None

    gather(
        bg,
        lambda ring, side: 4 * (ring * 2 + side),
        x,
        h,
        x_peer[1],
        x_peer[3],
        h_peer,
        lambda j: bg.at[pl.ds(4 * gc + 2 * j, 2)],
        no_forward,
        (mid_gather, late_gather),
    )
    sum_z()

    multiply(4, bg, True, BWD_PAIRS)
    sum_p()

    def cols_at(d, other):
        return ((z + d) % 4) * 2 + ((1 - a) if other else a)

    def block_of(d, other, core_):
        return 4 * (((1 - a) if other else a) * 8 + ((z + d) % 4) * 2 + core_)

    to_sib = {}
    for other in (1, 0):
        for d in (2, 1, 3, 0):
            shard = cols_at(d, other)
            for j in range(4):
                csend[shard, pl.ds(128 * j, 128), :] = prods[
                    meta[7, block_of(d, other, 1 - core) + j]
                ]
            to_sib[d, other] = net.put(csend.at[shard], crecv.at[shard], sib)

    def cols_ready(d, other):
        shard = cols_at(d, other)
        to_sib[d, other].wait_recv()
        for j in range(4):
            rows = pl.ds(128 * j, 128)
            mine = prods[meta[7, block_of(d, other, core) + j]].astype(f32)
            csum[shard, rows, :] = (mine + crecv[shard, rows, :].astype(f32)).astype(bf16)

    def mid_scatter():
        sum_h()

    def late_scatter():
        share_z()

    scatter(bwd_bufs, csum, cols_at, z, a, z_peer, a_peer, cols_ready, (mid_scatter, late_scatter))
    share_x()
    gfeat_out[...] = (own_part[...] + total[...]).astype(bf16)
    share_sib()
    for copy in state["gs"]:
        copy.wait_recv()
    gself_out[...] = wfull[0:256, :] * (1.0 / 256.0)
    gneigh_out[...] = wfull[256:512, :] * (1.0 / 256.0)
    net.finish()


def layer(meta, features, tiles, w_self, w_neigh, bias, cotangent):
    low = 512 - SPLIT_ROWS
    scatter_bufs = [
        VMEM((6, SPLIT_ROWS, 256), bf16),
        VMEM((4, low, 256), bf16),
        VMEM((SPLIT_ROWS, 256), bf16),
        VMEM((SPLIT_ROWS, 256), bf16),
        VMEM((3, low, 256), bf16),
        VMEM((3, low, 256), bf16),
    ]
    scratch = [
        VMEM((SLOTS + 1, 128, 128), bf16),
        VMEM((COL_BLOCKS, 128, 256), bf16),
        VMEM((BWD_PAIRS + 1, 128, 256), bf16),
        VMEM((128, 256), f32),
        VMEM((FWD_PAIRS + 1, 8, 128), f32),
        VMEM((8, 8, 128), f32),
        VMEM((8, 8, 128), f32),
        VMEM((8, 512, 256), bf16),
        VMEM((ROW_BLOCKS, 128, 256), bf16),
        VMEM((8, 512, 256), bf16),
        VMEM((8, 512, 256), bf16),
        VMEM((8, 512, 256), bf16),
        scatter_bufs,
        scatter_bufs,
        VMEM((512, 256), f32),
        VMEM((512, 256), f32),
        VMEM((256, 256), bf16),
        VMEM((256, 256), bf16),
        VMEM((512, 256), bf16),
        VMEM((512, 256), bf16),
        VMEM((512, 256), bf16),
        VMEM((512, 256), f32),
        VMEM((256, 256), f32),
        VMEM((64, 256), f32),
        VMEM((16, 256), f32),
        VMEM((8, 256), f32),
        VMEM((8, 256), f32),
        VMEM((4, 8, 256), f32),
        VMEM((256, 256), f32),
        VMEM((3, 64, 256), f32),
        VMEM((3, 16, 256), f32),
        VMEM((8, 256), f32),
        VMEM((8, 256), f32),
        VMEM((9, 8, 256), f32),
        VMEM((512, 256), f32),
        pltpu.SemaphoreType.DMA((SEMS,)),
        pltpu.SemaphoreType.DMA((SEMS,)),
        pltpu.SemaphoreType.DMA((5,)),
    ]
    anywhere = pl.BlockSpec(memory_space=pl.ANY)
    return pl.pallas_call(
        layer_kernel,
        out_shape=(
            jax.ShapeDtypeStruct((512, 256), bf16),
            jax.ShapeDtypeStruct((512, 256), bf16),
            jax.ShapeDtypeStruct((256, 256), f32),
            jax.ShapeDtypeStruct((256, 256), f32),
            jax.ShapeDtypeStruct((1, 256), f32),
        ),
        in_specs=[
            pl.BlockSpec(memory_space=SMEM),
            anywhere,
            anywhere,
            anywhere,
            anywhere,
            pl.BlockSpec(memory_space=VMEM),
            anywhere,
        ],
        out_specs=[pl.BlockSpec(memory_space=VMEM)] * 5,
        scratch_shapes=scratch,
        compiler_params=pltpu.CompilerParams(
            collective_id=0, has_side_effects=True, vmem_limit_bytes=60 * 1024 * 1024
        ),
        name="layer",
    )(meta, features, tiles, w_self, w_neigh, bias, cotangent)


def local(
    features,
    block_values,
    block_row,
    block_col,
    block_count,
    weight_self,
    weight_neigh,
    bias,
    cotangent,
):
    meta = plan(block_row, block_col, block_count)
    activations, grad_features, grad_self, grad_neigh, grad_bias = layer(
        meta,
        features.reshape(4, 128, 256),
        block_values.reshape(SLOTS, 128, 128),
        weight_self,
        weight_neigh,
        bias.reshape(1, 256),
        cotangent,
    )
    return (activations, grad_features, grad_self, grad_neigh, grad_bias.reshape(256))


def solution(mesh):
    placed = (
        P(("gr", "gc"), None),
        P("gr", "gc", None, None, None),
        P("gr", "gc", None),
        P("gr", "gc", None),
        P("gr", "gc"),
        P(),
        P(),
        P(),
        P(("gr", "gc"), None),
    )
    return jax.shard_map(
        local,
        mesh=mesh,
        in_specs=placed,
        out_specs=(P(("gr", "gc"), None), P(("gr", "gc"), None), P(), P(), P()),
        check_vma=False,
    )
```

```python
import functools

import jax
import jax.numpy as jnp
from jax import lax
from jax.experimental import pallas as pl
from jax.experimental.pallas import tpu as pltpu
from jax.sharding import PartitionSpec as P

MESH = pl.DeviceIdType.MESH
VMEM = pltpu.VMEM
SMEM = pltpu.SMEM

SLOTS = 384
ROW_BLOCKS = 32
COL_BLOCKS = 64
FWD_PAIRS = 208
BWD_PAIRS = 224
FWD_UNROLL = 26
BWD_UNROLL = 28
SPLIT_ROWS = 208
SEMS = 192
bf16, f32, i32 = jnp.bfloat16, jnp.float32, jnp.int32


def count_where(mask, axis, values=1):
    return jnp.sum(jnp.where(mask, values, 0), axis=axis, keepdims=True, dtype=i32)


def order_slots(key_lane, key_sub, other_sub, count, keys, others, empty):
    lane = lax.broadcasted_iota(i32, (1, SLOTS), 1)
    sub = lax.broadcasted_iota(i32, (SLOTS, 1), 0)
    key_l = jnp.where(lane < count, key_lane, -1)
    key_s = jnp.where(sub < count, key_sub, -2)
    rank = count_where((key_s == key_l) & (lane < sub), 1)
    k_lane = lax.broadcasted_iota(i32, (1, 128), 1)
    k_sub = lax.broadcasted_iota(i32, (keys, 1), 0)
    pairs_l = (count_where(key_s == k_lane, 0) + 1) >> 1
    pairs_s = (count_where(key_l == k_sub, 1) + 1) >> 1
    begin = count_where(k_lane < key_s, 1, pairs_l)
    place = jnp.where(sub < count, 2 * begin + rank, -1)
    begin_s = count_where(k_lane < k_sub, 1, pairs_l)
    begin_l = count_where(k_sub < k_lane, 0, pairs_s)
    spot = lax.broadcasted_iota(i32, (1, 512), 1)
    here = place == spot
    slot = SLOTS - count_where(here, 0, SLOTS - sub)
    other = count_where(here, 0, other_sub)
    first = (begin_s == spot) & (pairs_s > 0)
    keep = 1 - count_where(first, 0)
    last = jnp.where(pairs_l > 0, begin_l + pairs_l - 1, empty)
    last = jnp.concatenate([last] * 4, axis=1)
    slot = jnp.clip(slot, 0, SLOTS)
    other = jnp.clip(other, 0, others - 1)
    last = jnp.clip(last, 0, empty)
    return jnp.concatenate([slot, other, keep, last], axis=0)


def as_column(row):
    return jnp.broadcast_to(row, (128, SLOTS)).T[:, 0:1]


class Net:
    def __init__(self, send, recv):
        self.send, self.recv, self.started = send, recv, []

    def put(self, src, dst, device):
        at = len(self.started)
        copy = pltpu.make_async_remote_copy(
            src_ref=src,
            dst_ref=dst,
            send_sem=self.send.at[at],
            recv_sem=self.recv.at[at],
            device_id=device,
            device_id_type=MESH,
        )
        copy.start()
        self.started.append(copy)
        return copy

    def finish(self):
        assert len(self.started) <= SEMS
        for copy in self.started:
            copy.wait_send()


def layer_kernel(
    count_ref,
    row_ref,
    col_ref,
    feats,
    tiles_hbm,
    w_self_hbm,
    w_neigh_hbm,
    bias_ref,
    cot_hbm,
    act_out,
    gfeat_out,
    gweight_out,
    gbias_out,
    meta_v,
    meta,
    act_v,
    gfeat_v,
    tiles,
    xg,
    prods,
    acc,
    degp,
    degs,
    degr,
    rowsum,
    bg,
    csend,
    crecv,
    csum,
    fwd_bufs,
    bwd_bufs,
    total,
    own_part,
    w_self,
    w_neigh,
    cot,
    neigh,
    grad_pre,
    wg,
    w1,
    w2,
    w3,
    w4,
    bias0,
    bias_s,
    rs_,
    rx_,
    rz_,
    rp_,
    rh_,
    rb_,
    wfull,
    send_sem,
    recv_sem,
    local_sem,
):
    gr, gc = lax.axis_index("gr"), lax.axis_index("gc")
    a, z, core = gr // 8, (gr // 2) % 4, gr % 2
    x, h = gc // 2, gc % 2

    def device(a_=None, z_=None, core_=None, x_=None, h_=None):
        a_ = a if a_ is None else a_
        z_ = z if z_ is None else z_
        core_ = core if core_ is None else core_
        x_ = x if x_ is None else x_
        h_ = h if h_ is None else h_
        return (a_ * 8 + z_ * 2 + core_, x_ * 2 + h_)

    sib = device(core_=1 - core)
    z_peer = {d: device(z_=(z + d) % 4) for d in (1, 2, 3)}
    x_peer = {d: device(x_=(x + d) % 4) for d in (1, 2, 3)}
    a_peer = device(a_=1 - a)
    h_peer = device(h_=1 - h)
    diagonal = {d: device(x_=(x + d) % 4, h_=1 - h) for d in (1, 2, 3)}

    loads = [
        pltpu.make_async_copy(tiles_hbm, tiles.at[pl.ds(0, SLOTS)], local_sem.at[0]),
        pltpu.make_async_copy(feats, xg.at[pl.ds(4 * gr, 4)], local_sem.at[1]),
        pltpu.make_async_copy(w_self_hbm, w_self, local_sem.at[2]),
        pltpu.make_async_copy(w_neigh_hbm, w_neigh, local_sem.at[3]),
        pltpu.make_async_copy(cot_hbm, cot, local_sem.at[4]),
    ]
    for copy in loads:
        copy.start()

    barrier = pltpu.get_barrier_semaphore()
    peers = [sib, a_peer, h_peer]
    peers += list(z_peer.values()) + list(x_peer.values()) + list(diagonal.values())
    for peer in peers:
        pl.semaphore_signal(barrier, inc=1, device_id=peer, device_id_type=MESH)
    pl.semaphore_wait(barrier, len(peers))
    net = Net(send_sem, recv_sem)

    def gather(buf, base, ring, side, ring_peer, across, own, forward, steps):
        def piece(d, other, j, size=1):
            return buf.at[pl.ds(base((ring + d) % 4, (1 - side) if other else side) + j, size)]

        def push(d, other, j, device_id):
            return net.put(piece(d, other, j), piece(d, other, j), device_id)

        come = {}
        for j in range(4):
            for d in (2, 0, 1, 3):
                target = ring_peer[d] if d else across
                come[(4 - d) % 4, 0 if d else 1, j] = net.put(own(j), piece(0, 0, j), target)
        steps[0]()
        come[3, 0, 0].wait_recv()
        come[3, 1, 0] = push(3, 0, 0, across)
        come[1, 0, 0].wait_recv()
        come[1, 1, 0] = push(1, 0, 0, across)
        steps[1]()
        for j in range(4):
            come[2, 0, j].wait_recv()
            come[2, 1, j] = push(2, 0, j, across)
            if j:
                come[0, 1, j].wait_recv()
                come[3, 1, j] = push(0, 1, j, ring_peer[1])
                come[1, 1, j] = push(0, 1, j, ring_peer[3])
        sent = [forward(0, 0), forward(2, 0)]
        come[0, 1, 0].wait_recv()
        sent.append(forward(0, 1))
        for d in (1, 3):
            for j in (1, 2, 3):
                come[d, 0, j].wait_recv()
            sent.append(forward(d, 0))
        steps[2]()
        for d in (1, 3, 2):
            for j in range(4):
                come[d, 1, j].wait_recv()
            sent.append(forward(d, 1))
        for copy in sent:
            if copy is not None:
                copy.wait_recv()

    def scatter(bufs, src, at, ring, side, ring_peer, across, ready, steps):
        ra_buf, rb_buf, r2a_src, r2a_buf, r2b_src, r2b_buf = bufs
        top, low = pl.ds(0, SPLIT_ROWS), pl.ds(SPLIT_ROWS, 512 - SPLIT_ROWS)
        near, far, far_b = {}, {}, {}
        for d in (2, 1, 3, 0):
            ready(d, 1)
            far_b[d] = net.put(src.at[at(d, 1), low], rb_buf.at[d], across)
            if d:
                far[d] = net.put(src.at[at(d, 1), top], ra_buf.at[2 * d - 2], ring_peer[d])
        for d in (2, 1, 3, 0):
            ready(d, 0)
            if d:
                near[d] = net.put(src.at[at(d, 0), top], ra_buf.at[2 * d - 1], ring_peer[d])
        steps[0]()
        second = {}
        for d in (2, 1, 3):
            far_b[d].wait_recv()
            part = src[at(d, 0), low].astype(f32) + rb_buf[d].astype(f32)
            r2b_src[d - 1] = part.astype(bf16)
            second[d] = net.put(r2b_src.at[d - 1], r2b_buf.at[d - 1], ring_peer[d])
        part = src[at(0, 1), top].astype(f32)
        for d in (1, 3, 2):
            far[d].wait_recv()
            part += ra_buf[2 * d - 2].astype(f32)
        r2a_src[...] = part.astype(bf16)
        second_a = net.put(r2a_src, r2a_buf, across)
        part = src[at(0, 0), top].astype(f32)
        for d in (1, 3, 2):
            near[d].wait_recv()
            part += ra_buf[2 * d - 1].astype(f32)
        total[top, :] = part
        steps[1]()
        far_b[0].wait_recv()
        part = src[at(0, 0), low].astype(f32) + rb_buf[0].astype(f32)
        steps[2]()
        second_a.wait_recv()
        total[top, :] += r2a_buf[...].astype(f32)
        for d in (1, 3, 2):
            second[d].wait_recv()
            part += r2b_buf[d - 1].astype(f32)
        total[low, :] = part

    def multiply(base, source, backward, unroll, begin, end):
        if begin == 0:
            acc[...] = jnp.zeros_like(acc)

        def body(step, carry):
            for u in range(unroll):
                p = step * unroll + u
                left = [tiles[meta[base, 2 * p + i]] for i in (0, 1)]
                right = jnp.concatenate([source[meta[base + 1, 2 * p + i]] for i in (0, 1)], axis=0)
                if backward:
                    left = jnp.concatenate(left, axis=0)
                    form = (((0,), (0,)), ((), ()))
                else:
                    left = jnp.concatenate(left, axis=1)
                    form = (((1,), (0,)), ((), ()))
                product = lax.dot_general(left, right, form, preferred_element_type=f32)
                running = product + jnp.where(meta[base + 2, p] != 0, acc[...], 0.0)
                acc[...] = running
                prods[p] = running.astype(bf16)
            return carry

        lax.fori_loop(begin, end, body, 0)

    def count_some(begin, end):
        ones = jnp.ones((8, 256), bf16)

        def body(step, carry):
            for u in range(FWD_UNROLL):
                p = step * FWD_UNROLL + u
                pair = jnp.concatenate([tiles[meta[0, 2 * p + i]] for i in (0, 1)], axis=1)
                present = jnp.where(pair != 0, jnp.ones((), bf16), jnp.zeros((), bf16))
                found = lax.dot_general(
                    ones, present, (((1,), (1,)), ((), ())), preferred_element_type=f32
                )
                running = found + jnp.where(meta[2, p] != 0, degp[FWD_PAIRS], 0.0)
                degp[FWD_PAIRS] = running
                degp[p] = running
            return carry

        lax.fori_loop(begin, end, body, 0)

    def make_plan():
        count = count_ref[0, 0]
        row_l, col_l = row_ref[...], col_ref[...]
        row_s, col_s = as_column(row_l), as_column(col_l)
        meta_v[0:4, :] = order_slots(row_l, row_s, col_s, count, ROW_BLOCKS, COL_BLOCKS, FWD_PAIRS)
        meta_v[4:8, :] = order_slots(col_l, col_s, row_s, count, COL_BLOCKS, ROW_BLOCKS, BWD_PAIRS)
        copy = pltpu.make_async_copy(meta_v, meta, local_sem.at[5])
        copy.start()
        tiles[SLOTS] = jnp.zeros((128, 128), bf16)
        prods[FWD_PAIRS] = jnp.zeros((128, 256), bf16)
        degp[FWD_PAIRS] = jnp.zeros((8, 128), f32)
        copy.wait()

    def count_first():
        loads[0].wait()
        loads[1].wait()
        count_some(0, 4)

    degree_copies = []

    def count_last():
        count_some(4, 8)
        degp[FWD_PAIRS] = jnp.zeros((8, 128), f32)
        sub = lax.broadcasted_iota(i32, (8, 128), 0)
        for g in range(8):
            rows = jnp.zeros((8, 128), f32)
            for j in range(4):
                rows = jnp.where(sub == j, degp[meta[3, 4 * g + j]], rows)
            degs[g] = rows
        for d in range(4):
            for e in (0, 1):
                if (d, e) == (0, 0):
                    continue
                target = h_peer if d == 0 else (diagonal[d] if e else x_peer[d])
                index = ((x + d) % 4) * 2 + ((1 - h) if e else h)
                degree_copies.append(net.put(degs.at[index], degr.at[2 * d + e], target))
        for copy in loads[2:]:
            copy.wait()
        for j in range(4):
            own_part[pl.ds(128 * j, 128), :] = (
                jnp.dot(xg[4 * gr + j], w_self[...], preferred_element_type=f32) + bias_ref[...]
            )

    def to_sibling(d, other):
        at = 4 * ((1 - a if other else a) * 8 + ((z + d) % 4) * 2 + core)
        return net.put(xg.at[pl.ds(at, 4)], xg.at[pl.ds(at, 4)], sib)

    gather(
        xg,
        lambda ring, side: 4 * (side * 8 + ring * 2 + core),
        z,
        a,
        z_peer,
        a_peer,
        lambda j: feats.at[pl.ds(j, 1)],
        to_sibling,
        (make_plan, count_first, count_last),
    )

    multiply(0, xg, False, FWD_UNROLL, 0, 8)

    def rows_at(d, other):
        return ((x + d) % 4) * 2 + ((1 - h) if other else h)

    def rows_ready(d, other):
        shard = rows_at(d, other)
        for j in range(4):
            rowsum[shard, pl.ds(128 * j, 128), :] = prods[meta[3, 4 * shard + j]]

    def nothing():
        pass

    scatter(fwd_bufs, rowsum, rows_at, x, h, x_peer, h_peer, rows_ready, (nothing,) * 3)

    degree = degs[gc]
    for copy in degree_copies:
        copy.wait_recv()
    for slot in range(1, 8):
        degree += degr[slot]
    degree = jnp.maximum(degree, 1.0)
    gathered = {}
    for j in range(4):
        rows = pl.ds(128 * j, 128)
        counts = jnp.broadcast_to(degree[j : j + 1, :], (128, 128)).T
        counts = jnp.concatenate([counts, counts], axis=1)
        mean = (total[rows, :] / counts).astype(bf16)
        neigh[rows, :] = mean
        preact = own_part[rows, :] + jnp.dot(mean, w_neigh[...], preferred_element_type=f32)
        sigma = jax.nn.sigmoid(preact)
        act_v[rows, :] = (preact * sigma).astype(bf16)
        grad = cot[rows, :].astype(f32) * sigma * (1.0 + preact * (1.0 - sigma))
        grad = grad.astype(bf16)
        grad_pre[rows, :] = grad
        projected = lax.dot_general(
            grad, w_neigh[...], (((1,), (1,)), ((), ())), preferred_element_type=f32
        )
        bg[4 * gc + j] = (projected / counts).astype(bf16)

    stores = [pltpu.make_async_copy(act_v, act_out, local_sem.at[6])]
    stores[0].start()

    contract_rows = (((0,), (0,)), ((), ()))
    state = {}

    def weight_grads():
        own = jnp.concatenate([xg[4 * gr + j] for j in range(4)], axis=0)
        grad = grad_pre[...]
        wg[0:256, :] = lax.dot_general(own, grad, contract_rows, preferred_element_type=f32)
        wg[256:512, :] = lax.dot_general(
            neigh[...], grad, contract_rows, preferred_element_type=f32
        )
        bias0[...] = jnp.broadcast_to(
            jnp.sum(grad.astype(f32), axis=0, keepdims=True), (8, 256)
        )
        state["s"] = [
            net.put(wg.at[pl.ds((1 - core) * 256, 256)], rs_, sib),
            net.put(bias0, rb_.at[0], sib),
        ]
        own_part[...] = lax.dot_general(
            grad, w_self[...], (((1,), (1,)), ((), ())), preferred_element_type=f32
        )

    def sum_sib():
        for copy in state["s"]:
            copy.wait_recv()
        w1[...] = wg[pl.ds(core * 256, 256), :] + rs_[...]
        bias_s[0] = bias0[...] + rb_[0]
        state["x"] = []
        for d in (2, 1, 3):
            src = w1.at[pl.ds(((x + d) % 4) * 64, 64)]
            state["x"].append(net.put(src, rx_.at[d - 1], x_peer[d]))
            state["x"].append(net.put(bias_s.at[0], rb_.at[d], x_peer[d]))

    def sum_x():
        for copy in state["x"]:
            copy.wait_recv()
        w2[...] = w1[pl.ds(x * 64, 64), :] + rx_[0] + rx_[1] + rx_[2]
        bias_s[1] = bias_s[0] + rb_[1] + rb_[2] + rb_[3]
        state["z"] = []
        for d in (2, 1, 3):
            src = w2.at[pl.ds(((z + d) % 4) * 16, 16)]
            state["z"].append(net.put(src, rz_.at[d - 1], z_peer[d]))
            state["z"].append(net.put(bias_s.at[1], rb_.at[3 + d], z_peer[d]))

    def sum_z():
        for copy in state["z"]:
            copy.wait_recv()
        w3[...] = w2[pl.ds(z * 16, 16), :] + rz_[0] + rz_[1] + rz_[2]
        bias_s[2] = bias_s[1] + rb_[4] + rb_[5] + rb_[6]
        state["p"] = [
            net.put(w3.at[pl.ds((1 - a) * 8, 8)], rp_, a_peer),
            net.put(bias_s.at[2], rb_.at[7], a_peer),
        ]

    def sum_p():
        for copy in state["p"]:
            copy.wait_recv()
        w4[...] = w3[pl.ds(a * 8, 8), :] + rp_[...]
        bias_s[3] = bias_s[2] + rb_[7]
        state["h"] = [net.put(w4, rh_, h_peer), net.put(bias_s.at[3], rb_.at[8], h_peer)]

    def share(rows, size, targets):
        part = wfull.at[pl.ds(rows, size)]
        return [net.put(part, part, target) for target in targets]

    def sum_h():
        for copy in state["h"]:
            copy.wait_recv()
        mine = pl.ds(core * 256 + x * 64 + z * 16 + a * 8, 8)
        wfull[mine, :] = (w4[...] + rh_[...]) * (1.0 / 256.0)
        gbias_out[...] = (bias_s[3] + rb_[8])[0:1, :] * (1.0 / 256.0)
        state["gp"] = share(core * 256 + x * 64 + z * 16 + a * 8, 8, [a_peer])

    def share_z():
        for copy in state["gp"]:
            copy.wait_recv()
        state["gz"] = share(core * 256 + x * 64 + z * 16, 16, list(z_peer.values()))

    def share_x():
        for copy in state["gz"]:
            copy.wait_recv()
        state["gx"] = share(core * 256 + x * 64, 64, list(x_peer.values()))

    def share_sib():
        for copy in state["gx"]:
            copy.wait_recv()
        state["gs"] = share(core * 256, 256, [sib])

    def no_forward(d, other):
        return None

    gather(
        bg,
        lambda ring, side: 4 * (ring * 2 + side),
        x,
        h,
        x_peer,
        h_peer,
        lambda j: bg.at[pl.ds(4 * gc + j, 1)],
        no_forward,
        (weight_grads, sum_sib, sum_x),
    )
    sum_z()

    prods[BWD_PAIRS] = jnp.zeros((128, 256), bf16)
    multiply(4, bg, True, BWD_UNROLL, 0, 4)
    sum_p()
    multiply(4, bg, True, BWD_UNROLL, 4, 8)
    sum_h()

    def cols_at(d, other):
        return ((z + d) % 4) * 2 + ((1 - a) if other else a)

    def block_of(d, other, core_):
        return 4 * (((1 - a) if other else a) * 8 + ((z + d) % 4) * 2 + core_)

    to_sib = {}
    for other in (1, 0):
        for d in (2, 1, 3, 0):
            shard = cols_at(d, other)
            for j in range(4):
                csend[shard, pl.ds(128 * j, 128), :] = prods[
                    meta[7, block_of(d, other, 1 - core) + j]
                ]
            to_sib[d, other] = net.put(csend.at[shard], crecv.at[shard], sib)

    def cols_ready(d, other):
        shard = cols_at(d, other)
        to_sib[d, other].wait_recv()
        for j in range(4):
            rows = pl.ds(128 * j, 128)
            mine = prods[meta[7, block_of(d, other, core) + j]].astype(f32)
            csum[shard, rows, :] = (mine + crecv[shard, rows, :].astype(f32)).astype(bf16)

    def weights_out():
        for copy in state["gs"]:
            copy.wait_recv()
        stores.append(pltpu.make_async_copy(wfull, gweight_out, local_sem.at[7]))
        stores[1].start()

    share_z()
    scatter(
        bwd_bufs, csum, cols_at, z, a, z_peer, a_peer, cols_ready, (share_x, share_sib, weights_out)
    )
    gfeat_v[...] = (own_part[...] + total[...]).astype(bf16)
    stores.append(pltpu.make_async_copy(gfeat_v, gfeat_out, local_sem.at[8]))
    stores[2].start()
    net.finish()
    for copy in stores:
        copy.wait()


def layer(count, rows, cols, features, tiles, w_self, w_neigh, bias, cotangent):
    low = 512 - SPLIT_ROWS
    scatter_bufs = [
        VMEM((6, SPLIT_ROWS, 256), bf16),
        VMEM((4, low, 256), bf16),
        VMEM((SPLIT_ROWS, 256), bf16),
        VMEM((SPLIT_ROWS, 256), bf16),
        VMEM((3, low, 256), bf16),
        VMEM((3, low, 256), bf16),
    ]
    scratch = [
        VMEM((8, 512), i32),
        SMEM((8, 512), i32),
        VMEM((512, 256), bf16),
        VMEM((512, 256), bf16),
        VMEM((SLOTS + 1, 128, 128), bf16),
        VMEM((COL_BLOCKS, 128, 256), bf16),
        VMEM((BWD_PAIRS + 1, 128, 256), bf16),
        VMEM((128, 256), f32),
        VMEM((FWD_PAIRS + 1, 8, 128), f32),
        VMEM((8, 8, 128), f32),
        VMEM((8, 8, 128), f32),
        VMEM((8, 512, 256), bf16),
        VMEM((ROW_BLOCKS, 128, 256), bf16),
        VMEM((8, 512, 256), bf16),
        VMEM((8, 512, 256), bf16),
        VMEM((8, 512, 256), bf16),
        scatter_bufs,
        scatter_bufs,
        VMEM((512, 256), f32),
        VMEM((512, 256), f32),
        VMEM((256, 256), bf16),
        VMEM((256, 256), bf16),
        VMEM((512, 256), bf16),
        VMEM((512, 256), bf16),
        VMEM((512, 256), bf16),
        VMEM((512, 256), f32),
        VMEM((256, 256), f32),
        VMEM((64, 256), f32),
        VMEM((16, 256), f32),
        VMEM((8, 256), f32),
        VMEM((8, 256), f32),
        VMEM((4, 8, 256), f32),
        VMEM((256, 256), f32),
        VMEM((3, 64, 256), f32),
        VMEM((3, 16, 256), f32),
        VMEM((8, 256), f32),
        VMEM((8, 256), f32),
        VMEM((9, 8, 256), f32),
        VMEM((512, 256), f32),
        pltpu.SemaphoreType.DMA((SEMS,)),
        pltpu.SemaphoreType.DMA((SEMS,)),
        pltpu.SemaphoreType.DMA((9,)),
    ]
    anywhere = pl.BlockSpec(memory_space=pl.ANY)
    return pl.pallas_call(
        layer_kernel,
        out_shape=(
            jax.ShapeDtypeStruct((512, 256), bf16),
            jax.ShapeDtypeStruct((512, 256), bf16),
            jax.ShapeDtypeStruct((512, 256), f32),
            jax.ShapeDtypeStruct((1, 256), f32),
        ),
        in_specs=[pl.BlockSpec(memory_space=SMEM)]
        + [pl.BlockSpec(memory_space=VMEM)] * 2
        + [anywhere] * 4
        + [pl.BlockSpec(memory_space=VMEM), anywhere],
        out_specs=[anywhere] * 3 + [pl.BlockSpec(memory_space=VMEM)],
        scratch_shapes=scratch,
        compiler_params=pltpu.CompilerParams(
            collective_id=0, has_side_effects=True, vmem_limit_bytes=60 * 1024 * 1024
        ),
        name="layer",
    )(count, rows, cols, features, tiles, w_self, w_neigh, bias, cotangent)


def hand_over_kernel(act, gfeat, gweight, gbias, act_out, gfeat_out, gself, gneigh, gbias_out):
    act_out[...] = act[...]
    gfeat_out[...] = gfeat[...]
    gself[...] = gweight[0:256, :]
    gneigh[...] = gweight[256:512, :]
    gbias_out[...] = gbias[0, :]


def hand_over(act, gfeat, gweight, gbias):
    whole = pl.BlockSpec(memory_space=VMEM)
    return pl.pallas_call(
        hand_over_kernel,
        out_shape=(
            jax.ShapeDtypeStruct((512, 256), bf16),
            jax.ShapeDtypeStruct((512, 256), bf16),
            jax.ShapeDtypeStruct((256, 256), f32),
            jax.ShapeDtypeStruct((256, 256), f32),
            jax.ShapeDtypeStruct((256,), f32),
        ),
        in_specs=[whole] * 4,
        out_specs=[whole] * 5,
        compiler_params=pltpu.CompilerParams(vmem_limit_bytes=60 * 1024 * 1024),
        name="hand_over",
    )(act, gfeat, gweight, gbias)


def local(
    features,
    block_values,
    block_row,
    block_col,
    block_count,
    weight_self,
    weight_neigh,
    bias,
    cotangent,
):
    results = layer(
        block_count,
        block_row.reshape(1, SLOTS),
        block_col.reshape(1, SLOTS),
        features.reshape(4, 128, 256),
        block_values.reshape(SLOTS, 128, 128),
        weight_self,
        weight_neigh,
        bias.reshape(1, 256),
        cotangent,
    )
    return hand_over(*results)


def solution(mesh):
    placed = (
        P(("gr", "gc"), None),
        P("gr", "gc", None, None, None),
        P("gr", "gc", None),
        P("gr", "gc", None),
        P("gr", "gc"),
        P(),
        P(),
        P(),
        P(("gr", "gc"), None),
    )
    return jax.shard_map(
        local,
        mesh=mesh,
        in_specs=placed,
        out_specs=(P(("gr", "gc"), None), P(("gr", "gc"), None), P(), P(), P()),
        check_vma=False,
    )
```

```python
import functools

import jax
import jax.numpy as jnp
from jax import lax
from jax.experimental import pallas as pl
from jax.experimental.pallas import tpu as pltpu
from jax.sharding import PartitionSpec as P

MESH = pl.DeviceIdType.MESH
VMEM = pltpu.VMEM
SMEM = pltpu.SMEM

SLOTS = 384
ROW_BLOCKS = 32
COL_BLOCKS = 64
FWD_PAIRS = 208
BWD_PAIRS = 224
FWD_UNROLL = 26
BWD_UNROLL = 28
SPLIT_ROWS = 208
SEMS = 192
bf16, f32, i32 = jnp.bfloat16, jnp.float32, jnp.int32


def count_where(mask, axis, values=1):
    return jnp.sum(jnp.where(mask, values, 0), axis=axis, keepdims=True, dtype=i32)


def order_slots(key_lane, key_sub, other_sub, count, keys, others, empty):
    lane = lax.broadcasted_iota(i32, (1, SLOTS), 1)
    sub = lax.broadcasted_iota(i32, (SLOTS, 1), 0)
    key_l = jnp.where(lane < count, key_lane, -1)
    key_s = jnp.where(sub < count, key_sub, -2)
    rank = count_where((key_s == key_l) & (lane < sub), 1)
    k_lane = lax.broadcasted_iota(i32, (1, 128), 1)
    k_sub = lax.broadcasted_iota(i32, (keys, 1), 0)
    pairs_l = (count_where(key_s == k_lane, 0) + 1) >> 1
    pairs_s = (count_where(key_l == k_sub, 1) + 1) >> 1
    begin = count_where(k_lane < key_s, 1, pairs_l)
    place = jnp.where(sub < count, 2 * begin + rank, -1)
    begin_s = count_where(k_lane < k_sub, 1, pairs_l)
    begin_l = count_where(k_sub < k_lane, 0, pairs_s)
    spot = lax.broadcasted_iota(i32, (1, 512), 1)
    here = place == spot
    slot = SLOTS - count_where(here, 0, SLOTS - sub)
    other = count_where(here, 0, other_sub)
    first = (begin_s == spot) & (pairs_s > 0)
    keep = 1 - count_where(first, 0)
    last = jnp.where(pairs_l > 0, begin_l + pairs_l - 1, empty)
    last = jnp.concatenate([last] * 4, axis=1)
    slot = jnp.clip(slot, 0, SLOTS)
    other = jnp.clip(other, 0, others - 1)
    last = jnp.clip(last, 0, empty)
    return jnp.concatenate([slot, other, keep, last], axis=0)


def as_column(row):
    return jnp.broadcast_to(row, (128, SLOTS)).T[:, 0:1]


class Net:
    def __init__(self, send, recv):
        self.send, self.recv, self.started = send, recv, []

    def put(self, src, dst, device):
        at = len(self.started)
        copy = pltpu.make_async_remote_copy(
            src_ref=src,
            dst_ref=dst,
            send_sem=self.send.at[at],
            recv_sem=self.recv.at[at],
            device_id=device,
            device_id_type=MESH,
        )
        copy.start()
        self.started.append(copy)
        return copy

    def finish(self):
        assert len(self.started) <= SEMS
        for copy in self.started:
            copy.wait_send()


def layer_kernel(
    count_ref,
    row_ref,
    col_ref,
    feats,
    tiles_hbm,
    w_self_hbm,
    w_neigh_hbm,
    bias_ref,
    cot_hbm,
    act_out,
    gfeat_out,
    gweight_out,
    gbias_out,
    meta_v,
    meta,
    act_v,
    gfeat_v,
    tiles,
    xg,
    prods,
    acc,
    degp,
    degs,
    degr,
    rowsum,
    bg,
    csend,
    crecv,
    csum,
    fwd_bufs,
    bwd_bufs,
    total,
    total_back,
    own_part,
    w_self,
    w_neigh,
    cot,
    neigh,
    grad_pre,
    wg,
    rs_,
    w1,
    rx_,
    w2,
    rz_,
    wfull,
    send_sem,
    recv_sem,
    local_sem,
):
    gr, gc = lax.axis_index("gr"), lax.axis_index("gc")
    a, z, core = gr // 8, (gr // 2) % 4, gr % 2
    x, h = gc // 2, gc % 2

    def device(a_=None, z_=None, core_=None, x_=None, h_=None):
        a_ = a if a_ is None else a_
        z_ = z if z_ is None else z_
        core_ = core if core_ is None else core_
        x_ = x if x_ is None else x_
        h_ = h if h_ is None else h_
        return (a_ * 8 + z_ * 2 + core_, x_ * 2 + h_)

    sib = device(core_=1 - core)
    z_peer = {d: device(z_=(z + d) % 4) for d in (1, 2, 3)}
    x_peer = {d: device(x_=(x + d) % 4) for d in (1, 2, 3)}
    a_peer = device(a_=1 - a)
    h_peer = device(h_=1 - h)
    diagonal = {d: device(x_=(x + d) % 4, h_=1 - h) for d in (1, 2, 3)}
    z_diagonal = {d: device(z_=(z + d) % 4, a_=1 - a) for d in (1, 2, 3)}
    far_first = (2, 1, 3, 0)
    row_peers = [(((x + d) % 4) * 2 + 1 - h, diagonal[d] if d else h_peer) for d in far_first]
    row_peers += [(((x + d) % 4) * 2 + h, x_peer[d]) for d in far_first if d]
    col_peers = [z_diagonal[d] if d else a_peer for d in far_first]
    col_peers += [z_peer[d] for d in far_first if d]

    loads = [
        pltpu.make_async_copy(
            feats.at[:, :, pl.ds(128 * f, 128)], xg[f].at[pl.ds(4 * gr, 4)], local_sem.at[f]
        )
        for f in (0, 1)
    ]
    loads += [
        pltpu.make_async_copy(tiles_hbm, tiles.at[pl.ds(0, SLOTS)], local_sem.at[2]),
        pltpu.make_async_copy(w_self_hbm, w_self, local_sem.at[3]),
        pltpu.make_async_copy(w_neigh_hbm, w_neigh, local_sem.at[4]),
        pltpu.make_async_copy(cot_hbm, cot, local_sem.at[5]),
    ]
    for copy in loads:
        copy.start()

    barrier = pltpu.get_barrier_semaphore()
    peers = [sib, a_peer, h_peer]
    peers += list(z_peer.values()) + list(x_peer.values()) + list(diagonal.values())
    peers += list(z_diagonal.values())
    for peer in peers:
        pl.semaphore_signal(barrier, inc=1, device_id=peer, device_id_type=MESH)
    loads[0].wait()
    loads[1].wait()
    pl.semaphore_wait(barrier, len(peers))
    net = Net(send_sem, recv_sem)

    def gather(buf, base, ring, side, ring_peer, across, forward):
        def push(d, other, j, device_id):
            at = base((ring + d) % 4, (1 - side) if other else side) + j
            piece = buf.at[pl.ds(at, 1)]
            return net.put(piece, piece, device_id)

        near, far = {}, {}
        for j in range(4):
            for d in (2, 0, 1, 3):
                near[(4 - d) % 4, j] = push(0, 0, j, ring_peer[d] if d else across)
        sent = [forward(0, 0)]
        yield
        for d in (3, 1):
            near[d, 0].wait_recv()
            far[d, 0] = push(d, 0, 0, across)
        yield
        for j in range(4):
            near[2, j].wait_recv()
            far[2, j] = push(2, 0, j, across)
            if j:
                near[0, j].wait_recv()
                far[3, j] = push(0, 1, j, ring_peer[1])
                far[1, j] = push(0, 1, j, ring_peer[3])
        yield
        near[0, 0].wait_recv()
        for d in (1, 3):
            for j in (1, 2, 3):
                near[d, j].wait_recv()
        sent += [forward(0, 1), forward(1, 0), forward(3, 0), forward(2, 0)]
        yield
        for d in (1, 3, 2):
            for j in range(4):
                far[d, j].wait_recv()
            sent.append(forward(d, 1))
        for copy in sent:
            if copy is not None:
                copy.wait_recv()
        yield

    def scatter(bufs, src, out, at, ring, side, ring_peer, across, ready):
        ra_buf, rb_buf, r2a_src, r2a_buf, r2b_src, r2b_buf = bufs
        top, low = pl.ds(0, SPLIT_ROWS), pl.ds(SPLIT_ROWS, 512 - SPLIT_ROWS)
        near, far, far_b = {}, {}, {}
        for d in (2, 1, 3, 0):
            ready(d, 1)
            far_b[d] = net.put(src.at[at(d, 1), low], rb_buf.at[d], across)
            if d:
                far[d] = net.put(src.at[at(d, 1), top], ra_buf.at[2 * d - 2], ring_peer[d])
        for d in (2, 1, 3, 0):
            ready(d, 0)
            if d:
                near[d] = net.put(src.at[at(d, 0), top], ra_buf.at[2 * d - 1], ring_peer[d])
        yield
        second = {}
        for d in (2, 1, 3):
            far_b[d].wait_recv()
            part = src[at(d, 0), low].astype(f32) + rb_buf[d].astype(f32)
            r2b_src[d - 1] = part.astype(bf16)
            second[d] = net.put(r2b_src.at[d - 1], r2b_buf.at[d - 1], ring_peer[d])
        part = src[at(0, 1), top].astype(f32)
        for d in (1, 3, 2):
            far[d].wait_recv()
            part += ra_buf[2 * d - 2].astype(f32)
        r2a_src[...] = part.astype(bf16)
        second_a = net.put(r2a_src, r2a_buf, across)
        yield
        part = src[at(0, 0), top].astype(f32)
        for d in (1, 3, 2):
            near[d].wait_recv()
            part += ra_buf[2 * d - 1].astype(f32)
        out[top, :] = part
        far_b[0].wait_recv()
        out[low, :] = src[at(0, 0), low].astype(f32) + rb_buf[0].astype(f32)
        yield
        second_a.wait_recv()
        out[top, :] += r2a_buf[...].astype(f32)
        part = out[low, :]
        for d in (1, 3, 2):
            second[d].wait_recv()
            part += r2b_buf[d - 1].astype(f32)
        out[low, :] = part
        yield

    def multiply(base, source, lanes, backward, unroll, begin, end):
        if begin == 0:
            acc[:, lanes] = jnp.zeros_like(acc[:, lanes])

        def body(step, carry):
            for u in range(unroll):
                p = step * unroll + u
                left = [tiles[meta[base, 2 * p + i]] for i in (0, 1)]
                right = [source[meta[base + 1, 2 * p + i]] for i in (0, 1)]
                right = jnp.concatenate(right, axis=0)
                if backward:
                    left = jnp.concatenate(left, axis=0)
                    form = (((0,), (0,)), ((), ()))
                else:
                    left = jnp.concatenate(left, axis=1)
                    form = (((1,), (0,)), ((), ()))
                product = lax.dot_general(left, right, form, preferred_element_type=f32)
                running = product + jnp.where(meta[base + 2, p] != 0, acc[:, lanes], 0.0)
                acc[:, lanes] = running
                prods[p, :, lanes] = running.astype(bf16)
            return carry

        lax.fori_loop(begin, end, body, 0)

    def count_some(begin, end):
        ones = jnp.ones((8, 256), bf16)

        def body(step, carry):
            for u in range(FWD_UNROLL):
                p = step * FWD_UNROLL + u
                pair = jnp.concatenate([tiles[meta[0, 2 * p + i]] for i in (0, 1)], axis=1)
                present = jnp.where(pair != 0, jnp.ones((), bf16), jnp.zeros((), bf16))
                found = lax.dot_general(
                    ones, present, (((1,), (1,)), ((), ())), preferred_element_type=f32
                )
                running = found + jnp.where(meta[2, p] != 0, degp[FWD_PAIRS], 0.0)
                degp[FWD_PAIRS] = running
                degp[p] = running
            return carry

        lax.fori_loop(begin, end, body, 0)

    def make_plan():
        count = count_ref[0, 0]
        row_l, col_l = row_ref[...], col_ref[...]
        row_s, col_s = as_column(row_l), as_column(col_l)
        meta_v[0:4, :] = order_slots(row_l, row_s, col_s, count, ROW_BLOCKS, COL_BLOCKS, FWD_PAIRS)
        meta_v[4:8, :] = order_slots(col_l, col_s, row_s, count, COL_BLOCKS, ROW_BLOCKS, BWD_PAIRS)
        copy = pltpu.make_async_copy(meta_v, meta, local_sem.at[9])
        copy.start()
        tiles[SLOTS] = jnp.zeros((128, 128), bf16)
        prods[FWD_PAIRS] = jnp.zeros((128, 256), bf16)
        degp[FWD_PAIRS] = jnp.zeros((8, 128), f32)
        copy.wait()

    degree_copies = []

    def count_last():
        degp[FWD_PAIRS] = jnp.zeros((8, 128), f32)
        sub = lax.broadcasted_iota(i32, (8, 128), 0)
        for g in range(8):
            rows = jnp.zeros((8, 128), f32)
            for j in range(4):
                rows = jnp.where(sub == j, degp[meta[3, 4 * g + j]], rows)
            degs[g] = rows
        for d in range(4):
            for e in (0, 1):
                if (d, e) == (0, 0):
                    continue
                target = h_peer if d == 0 else (diagonal[d] if e else x_peer[d])
                index = ((x + d) % 4) * 2 + ((1 - h) if e else h)
                degree_copies.append(net.put(degs.at[index], degr.at[2 * d + e], target))
        for copy in loads[3:]:
            copy.wait()
        for j in range(4):
            own = jnp.concatenate([xg[f][4 * gr + j] for f in (0, 1)], axis=1)
            own_part[pl.ds(128 * j, 128), :] = (
                jnp.dot(own, w_self[...], preferred_element_type=f32) + bias_ref[...]
            )

    def feature_gather(f):
        def to_sibling(d, other):
            at = 4 * ((1 - a if other else a) * 8 + ((z + d) % 4) * 2 + core)
            shard = xg[f].at[pl.ds(at, 4)]
            return net.put(shard, shard, sib)

        return gather(
            xg[f],
            lambda ring, side: 4 * (side * 8 + ring * 2 + core),
            z,
            a,
            z_peer,
            a_peer,
            to_sibling,
        )

    def rows_at(d, other):
        return ((x + d) % 4) * 2 + ((1 - h) if other else h)

    def row_scatter(f):
        def rows_ready(d, other):
            shard = rows_at(d, other)
            for j in range(4):
                rowsum[f, shard, pl.ds(128 * j, 128), :] = prods[
                    meta[3, 4 * shard + j], :, pl.ds(128 * f, 128)
                ]

        bufs = [buf.at[f] for buf in fwd_bufs]
        return scatter(
            bufs, rowsum.at[f], total.at[f], rows_at, x, h, x_peer, h_peer, rows_ready
        )

    def forward_part(f, begin, end):
        multiply(0, xg[f], pl.ds(128 * f, 128), False, FWD_UNROLL, begin, end)

    get = [feature_gather(0), feature_gather(1)]
    put = [row_scatter(0), row_scatter(1)]
    next(get[0])
    make_plan()
    loads[2].wait()
    next(get[0])
    count_some(0, 2)
    next(get[0])
    next(get[1])
    count_some(2, 6)
    next(get[0])
    count_some(6, 8)
    count_last()
    next(get[0])
    forward_part(0, 0, 2)
    next(get[1])
    forward_part(0, 2, 4)
    next(get[1])
    forward_part(0, 4, 6)
    next(get[1])
    forward_part(0, 6, 8)
    next(put[0])
    next(get[1])
    forward_part(1, 0, 8)
    next(put[0])
    next(put[1])
    next(put[0])
    next(put[1])
    next(put[0])
    next(put[1])
    next(put[1])

    degree = degs[gc]
    for copy in degree_copies:
        copy.wait_recv()
    for slot in range(1, 8):
        degree += degr[slot]
    degree = jnp.maximum(degree, 1.0)
    gathered = {}
    for j in range(4):
        rows = pl.ds(128 * j, 128)
        counts = jnp.broadcast_to(degree[j : j + 1, :], (128, 128)).T
        counts = jnp.concatenate([counts, counts], axis=1)
        summed = jnp.concatenate([total[f, rows, :] for f in (0, 1)], axis=1)
        mean = (summed / counts).astype(bf16)
        neigh[rows, :] = mean
        preact = own_part[rows, :] + jnp.dot(mean, w_neigh[...], preferred_element_type=f32)
        sigma = jax.nn.sigmoid(preact)
        act_v[rows, :] = (preact * sigma).astype(bf16)
        grad = cot[rows, :].astype(f32) * sigma * (1.0 + preact * (1.0 - sigma))
        grad = grad.astype(bf16)
        grad_pre[rows, :] = grad
        projected = lax.dot_general(
            grad, w_neigh[...], (((1,), (1,)), ((), ())), preferred_element_type=f32
        )
        bg[4 * gc + j] = (projected / counts).astype(bf16)

    stores = [pltpu.make_async_copy(act_v, act_out, local_sem.at[6])]
    stores[0].start()

    contract_rows = (((0,), (0,)), ((), ()))
    state = {}

    def weight_grads():
        grad = grad_pre[...]
        for f in (0, 1):
            own = jnp.concatenate([xg[f][4 * gr + j] for j in range(4)], axis=0)
            wg[0, pl.ds(128 * f, 128), :] = lax.dot_general(
                own, grad, contract_rows, preferred_element_type=f32
            )
        wg[1, 0:256, :] = lax.dot_general(
            neigh[...], grad, contract_rows, preferred_element_type=f32
        )
        bias = jnp.sum(grad.astype(f32), axis=0, keepdims=True)
        for side in (0, 1):
            wg[side, 256:264, :] = jnp.broadcast_to(bias, (8, 256))
        state["s"] = [net.put(wg.at[1 - core], rs_, sib)]
        own_part[...] = lax.dot_general(
            grad, w_self[...], (((1,), (1,)), ((), ())), preferred_element_type=f32
        )

    def sum_sib():
        for copy in state["s"]:
            copy.wait_recv()
        both = wg[core] + rs_[...]
        for g in range(8):
            w1[g, 0:32, :] = both[32 * g : 32 * g + 32, :]
            w1[g, 32:40, :] = both[256:264, :]
        rx_[gc] = w1[gc]
        state["x"] = [net.put(w1.at[to], rx_.at[gc], target) for to, target in row_peers]

    def sum_row():
        for copy in state["x"]:
            copy.wait_recv()
        part = rx_[0]
        for g in range(1, 8):
            part += rx_[g]
        w2[...] = part
        rz_[z * 2 + a] = part
        state["z"] = [net.put(w2, rz_.at[z * 2 + a], target) for target in col_peers]

    def sum_all():
        for copy in state["z"]:
            copy.wait_recv()
        part = rz_[0]
        for g in range(1, 8):
            part += rz_[g]
        mine = pl.ds(core * 256 + gc * 32, 32)
        wfull[mine, :] = part[0:32, :] * (1.0 / 256.0)
        gbias_out[...] = part[32:33, :] * (1.0 / 256.0)
        piece = wfull.at[mine]
        state["gx"] = [net.put(piece, piece, target) for _, target in row_peers]

    def share_sib():
        for copy in state["gx"]:
            copy.wait_recv()
        half = wfull.at[pl.ds(core * 256, 256)]
        state["gs"] = [net.put(half, half, sib)]

    def no_forward(d, other):
        return None

    def cols_at(d, other):
        return ((z + d) % 4) * 2 + ((1 - a) if other else a)

    def block_of(d, other, core_):
        return 4 * (((1 - a) if other else a) * 8 + ((z + d) % 4) * 2 + core_)

    to_sib = {}

    def cols_to_sibling():
        for other in (1, 0):
            for d in (2, 1, 3, 0):
                shard = cols_at(d, other)
                for j in range(4):
                    csend[shard, pl.ds(128 * j, 128), :] = prods[
                        meta[7, block_of(d, other, 1 - core) + j]
                    ]
                to_sib[d, other] = net.put(csend.at[shard], crecv.at[shard], sib)

    def cols_ready(d, other):
        shard = cols_at(d, other)
        to_sib[d, other].wait_recv()
        for j in range(4):
            rows = pl.ds(128 * j, 128)
            mine = prods[meta[7, block_of(d, other, core) + j]].astype(f32)
            csum[shard, rows, :] = (mine + crecv[shard, rows, :].astype(f32)).astype(bf16)

    def weights_out():
        for copy in state["gs"]:
            copy.wait_recv()
        stores.append(pltpu.make_async_copy(wfull, gweight_out, local_sem.at[7]))
        stores[1].start()

    get = gather(bg, lambda ring, side: 4 * (ring * 2 + side), x, h, x_peer, h_peer, no_forward)
    put = scatter(bwd_bufs, csum, total_back, cols_at, z, a, z_peer, a_peer, cols_ready)
    every = pl.ds(0, 256)
    next(get)
    next(get)
    next(get)
    weight_grads()
    next(get)
    next(get)
    sum_sib()
    prods[BWD_PAIRS] = jnp.zeros((128, 256), bf16)
    multiply(4, bg, every, True, BWD_UNROLL, 0, 4)
    sum_row()
    multiply(4, bg, every, True, BWD_UNROLL, 4, 8)
    cols_to_sibling()
    sum_all()
    next(put)
    next(put)
    share_sib()
    next(put)
    weights_out()
    next(put)
    gfeat_v[...] = (own_part[...] + total_back[...]).astype(bf16)
    stores.append(pltpu.make_async_copy(gfeat_v, gfeat_out, local_sem.at[8]))
    stores[2].start()
    net.finish()
    for copy in stores:
        copy.wait()


def layer(count, rows, cols, features, tiles, w_self, w_neigh, bias, cotangent):
    low = 512 - SPLIT_ROWS
    def scatter_bufs(*lead, width):
        return [
            VMEM((*lead, 6, SPLIT_ROWS, width), bf16),
            VMEM((*lead, 4, low, width), bf16),
            VMEM((*lead, SPLIT_ROWS, width), bf16),
            VMEM((*lead, SPLIT_ROWS, width), bf16),
            VMEM((*lead, 3, low, width), bf16),
            VMEM((*lead, 3, low, width), bf16),
        ]

    scratch = [
        VMEM((8, 512), i32),
        SMEM((8, 512), i32),
        VMEM((512, 256), bf16),
        VMEM((512, 256), bf16),
        VMEM((SLOTS + 1, 128, 128), bf16),
        [VMEM((COL_BLOCKS, 128, 128), bf16)] * 2,
        VMEM((BWD_PAIRS + 1, 128, 256), bf16),
        VMEM((128, 256), f32),
        VMEM((FWD_PAIRS + 1, 8, 128), f32),
        VMEM((8, 8, 128), f32),
        VMEM((8, 8, 128), f32),
        VMEM((2, 8, 512, 128), bf16),
        VMEM((ROW_BLOCKS, 128, 256), bf16),
        VMEM((8, 512, 256), bf16),
        VMEM((8, 512, 256), bf16),
        VMEM((8, 512, 256), bf16),
        scatter_bufs(2, width=128),
        scatter_bufs(width=256),
        VMEM((2, 512, 128), f32),
        VMEM((512, 256), f32),
        VMEM((512, 256), f32),
        VMEM((256, 256), bf16),
        VMEM((256, 256), bf16),
        VMEM((512, 256), bf16),
        VMEM((512, 256), bf16),
        VMEM((512, 256), bf16),
        VMEM((2, 264, 256), f32),
        VMEM((264, 256), f32),
        VMEM((8, 40, 256), f32),
        VMEM((8, 40, 256), f32),
        VMEM((40, 256), f32),
        VMEM((8, 40, 256), f32),
        VMEM((512, 256), f32),
        pltpu.SemaphoreType.DMA((SEMS,)),
        pltpu.SemaphoreType.DMA((SEMS,)),
        pltpu.SemaphoreType.DMA((10,)),
    ]
    anywhere = pl.BlockSpec(memory_space=pl.ANY)
    return pl.pallas_call(
        layer_kernel,
        out_shape=(
            jax.ShapeDtypeStruct((512, 256), bf16),
            jax.ShapeDtypeStruct((512, 256), bf16),
            jax.ShapeDtypeStruct((512, 256), f32),
            jax.ShapeDtypeStruct((1, 256), f32),
        ),
        in_specs=[pl.BlockSpec(memory_space=SMEM)]
        + [pl.BlockSpec(memory_space=VMEM)] * 2
        + [anywhere] * 4
        + [pl.BlockSpec(memory_space=VMEM), anywhere],
        out_specs=[anywhere] * 3 + [pl.BlockSpec(memory_space=VMEM)],
        scratch_shapes=scratch,
        compiler_params=pltpu.CompilerParams(
            collective_id=0, has_side_effects=True, vmem_limit_bytes=60 * 1024 * 1024
        ),
        name="layer",
    )(count, rows, cols, features, tiles, w_self, w_neigh, bias, cotangent)


def hand_over_kernel(act, gfeat, gweight, gbias, act_out, gfeat_out, gself, gneigh, gbias_out):
    act_out[...] = act[...]
    gfeat_out[...] = gfeat[...]
    gself[...] = gweight[0:256, :]
    gneigh[...] = gweight[256:512, :]
    gbias_out[...] = gbias[0, :]


def hand_over(act, gfeat, gweight, gbias):
    whole = pl.BlockSpec(memory_space=VMEM)
    return pl.pallas_call(
        hand_over_kernel,
        out_shape=(
            jax.ShapeDtypeStruct((512, 256), bf16),
            jax.ShapeDtypeStruct((512, 256), bf16),
            jax.ShapeDtypeStruct((256, 256), f32),
            jax.ShapeDtypeStruct((256, 256), f32),
            jax.ShapeDtypeStruct((256,), f32),
        ),
        in_specs=[whole] * 4,
        out_specs=[whole] * 5,
        compiler_params=pltpu.CompilerParams(vmem_limit_bytes=60 * 1024 * 1024),
        name="hand_over",
    )(act, gfeat, gweight, gbias)


def local(
    features,
    block_values,
    block_row,
    block_col,
    block_count,
    weight_self,
    weight_neigh,
    bias,
    cotangent,
):
    results = layer(
        block_count,
        block_row.reshape(1, SLOTS),
        block_col.reshape(1, SLOTS),
        features.reshape(4, 128, 256),
        block_values.reshape(SLOTS, 128, 128),
        weight_self,
        weight_neigh,
        bias.reshape(1, 256),
        cotangent,
    )
    return hand_over(*results)


def solution(mesh):
    placed = (
        P(("gr", "gc"), None),
        P("gr", "gc", None, None, None),
        P("gr", "gc", None),
        P("gr", "gc", None),
        P("gr", "gc"),
        P(),
        P(),
        P(),
        P(("gr", "gc"), None),
    )
    return jax.shard_map(
        local,
        mesh=mesh,
        in_specs=placed,
        out_specs=(P(("gr", "gc"), None), P(("gr", "gc"), None), P(), P(), P()),
        check_vma=False,
    )
```

```python
import functools

import jax
import jax.numpy as jnp
from jax import lax
from jax.experimental import pallas as pl
from jax.experimental.pallas import tpu as pltpu
from jax.sharding import PartitionSpec as P

MESH = pl.DeviceIdType.MESH
VMEM = pltpu.VMEM
SMEM = pltpu.SMEM

SLOTS = 384
ROW_BLOCKS = 32
COL_BLOCKS = 64
FWD_PAIRS = 208
BWD_PAIRS = 224
FWD_UNROLL = 26
BWD_UNROLL = 28
SPLIT_ROWS = 208
SEMS = 192
bf16, f32, i32 = jnp.bfloat16, jnp.float32, jnp.int32


def count_where(mask, axis, values=1):
    return jnp.sum(jnp.where(mask, values, 0), axis=axis, keepdims=True, dtype=i32)


def order_slots(key_lane, key_sub, other_sub, count, keys, others, empty):
    lane = lax.broadcasted_iota(i32, (1, SLOTS), 1)
    sub = lax.broadcasted_iota(i32, (SLOTS, 1), 0)
    key_l = jnp.where(lane < count, key_lane, -1)
    key_s = jnp.where(sub < count, key_sub, -2)
    rank = count_where((key_s == key_l) & (lane < sub), 1)
    k_lane = lax.broadcasted_iota(i32, (1, 128), 1)
    k_sub = lax.broadcasted_iota(i32, (keys, 1), 0)
    pairs_l = (count_where(key_s == k_lane, 0) + 1) >> 1
    pairs_s = (count_where(key_l == k_sub, 1) + 1) >> 1
    begin = count_where(k_lane < key_s, 1, pairs_l)
    place = jnp.where(sub < count, 2 * begin + rank, -1)
    begin_s = count_where(k_lane < k_sub, 1, pairs_l)
    begin_l = count_where(k_sub < k_lane, 0, pairs_s)
    spot = lax.broadcasted_iota(i32, (1, 512), 1)
    here = place == spot
    slot = SLOTS - count_where(here, 0, SLOTS - sub)
    other = count_where(here, 0, other_sub)
    first = (begin_s == spot) & (pairs_s > 0)
    keep = 1 - count_where(first, 0)
    last = jnp.where(pairs_l > 0, begin_l + pairs_l - 1, empty)
    last = jnp.concatenate([last] * 4, axis=1)
    slot = jnp.clip(slot, 0, SLOTS)
    other = jnp.clip(other, 0, others - 1)
    last = jnp.clip(last, 0, empty)
    return jnp.concatenate([slot, other, keep, last], axis=0)


def as_column(row):
    return jnp.broadcast_to(row, (128, SLOTS)).T[:, 0:1]


class Net:
    def __init__(self, send, recv):
        self.send, self.recv, self.started = send, recv, []

    def put(self, src, dst, device):
        at = len(self.started)
        copy = pltpu.make_async_remote_copy(
            src_ref=src,
            dst_ref=dst,
            send_sem=self.send.at[at],
            recv_sem=self.recv.at[at],
            device_id=device,
            device_id_type=MESH,
        )
        copy.start()
        self.started.append(copy)
        return copy

    def finish(self):
        assert len(self.started) <= SEMS
        for copy in self.started:
            copy.wait_send()


def layer_kernel(
    count_ref,
    row_ref,
    col_ref,
    feats,
    tiles_hbm,
    w_self_hbm,
    w_neigh_hbm,
    bias_ref,
    cot_hbm,
    act_out,
    gfeat_out,
    gweight_out,
    gbias_out,
    meta_v,
    meta,
    act_v,
    gfeat_v,
    tiles,
    xg,
    prods,
    acc,
    degp,
    degs,
    degr,
    rowsum,
    bg,
    csend,
    crecv,
    csum,
    fwd_bufs,
    bwd_bufs,
    total,
    total_back,
    own_part,
    w_self,
    w_neigh,
    cot,
    neigh,
    grad_pre,
    wg,
    rs_,
    w1,
    rx_,
    w2,
    rz_,
    wfull,
    send_sem,
    recv_sem,
    local_sem,
):
    gr, gc = lax.axis_index("gr"), lax.axis_index("gc")
    a, z, core = gr // 8, (gr // 2) % 4, gr % 2
    x, h = gc // 2, gc % 2

    def device(a_=None, z_=None, core_=None, x_=None, h_=None):
        a_ = a if a_ is None else a_
        z_ = z if z_ is None else z_
        core_ = core if core_ is None else core_
        x_ = x if x_ is None else x_
        h_ = h if h_ is None else h_
        return (a_ * 8 + z_ * 2 + core_, x_ * 2 + h_)

    sib = device(core_=1 - core)
    z_peer = {d: device(z_=(z + d) % 4) for d in (1, 2, 3)}
    x_peer = {d: device(x_=(x + d) % 4) for d in (1, 2, 3)}
    a_peer = device(a_=1 - a)
    h_peer = device(h_=1 - h)
    diagonal = {d: device(x_=(x + d) % 4, h_=1 - h) for d in (1, 2, 3)}
    z_diagonal = {d: device(z_=(z + d) % 4, a_=1 - a) for d in (1, 2, 3)}
    far_first = (2, 1, 3, 0)
    row_peers = [(((x + d) % 4) * 2 + 1 - h, diagonal[d] if d else h_peer) for d in far_first]
    row_peers += [(((x + d) % 4) * 2 + h, x_peer[d]) for d in far_first if d]
    col_peers = [z_diagonal[d] if d else a_peer for d in far_first]
    col_peers += [z_peer[d] for d in far_first if d]

    loads = [
        pltpu.make_async_copy(
            feats.at[:, :, pl.ds(128 * f, 128)], xg[f].at[pl.ds(4 * gr, 4)], local_sem.at[f]
        )
        for f in (0, 1)
    ]
    loads += [
        pltpu.make_async_copy(tiles_hbm, tiles.at[pl.ds(0, SLOTS)], local_sem.at[2]),
        pltpu.make_async_copy(w_self_hbm, w_self, local_sem.at[3]),
        pltpu.make_async_copy(w_neigh_hbm, w_neigh, local_sem.at[4]),
        pltpu.make_async_copy(cot_hbm, cot, local_sem.at[5]),
    ]
    for copy in loads:
        copy.start()

    barrier = pltpu.get_barrier_semaphore()
    peers = [sib, a_peer, h_peer]
    peers += list(z_peer.values()) + list(x_peer.values()) + list(diagonal.values())
    peers += list(z_diagonal.values())
    for peer in peers:
        pl.semaphore_signal(barrier, inc=1, device_id=peer, device_id_type=MESH)
    loads[0].wait()
    loads[1].wait()
    pl.semaphore_wait(barrier, len(peers))
    net = Net(send_sem, recv_sem)

    def gather(buf, base, ring, side, ring_peer, across, forward, make=None):
        def push(d, other, j, device_id):
            at = base((ring + d) % 4, (1 - side) if other else side) + j
            piece = buf.at[pl.ds(at, 1)]
            return net.put(piece, piece, device_id)

        near, far = {}, {}
        for j in range(4):
            if make is not None:
                make(j)
            for d in (2, 0, 1, 3):
                near[(4 - d) % 4, j] = push(0, 0, j, ring_peer[d] if d else across)
        sent = [forward(0, 0)]
        yield
        for d in (3, 1):
            near[d, 0].wait_recv()
            far[d, 0] = push(d, 0, 0, across)
        yield
        for j in range(4):
            near[2, j].wait_recv()
            far[2, j] = push(2, 0, j, across)
            if j:
                near[0, j].wait_recv()
                far[3, j] = push(0, 1, j, ring_peer[1])
                far[1, j] = push(0, 1, j, ring_peer[3])
        yield
        near[0, 0].wait_recv()
        for d in (1, 3):
            for j in (1, 2, 3):
                near[d, j].wait_recv()
        sent += [forward(0, 1), forward(1, 0), forward(3, 0), forward(2, 0)]
        yield
        for d in (1, 3, 2):
            for j in range(4):
                far[d, j].wait_recv()
            sent.append(forward(d, 1))
        for copy in sent:
            if copy is not None:
                copy.wait_recv()
        yield

    def scatter(bufs, src, out, at, ring, side, ring_peer, across, ready):
        ra_buf, rb_buf, r2a_src, r2a_buf, r2b_src, r2b_buf = bufs
        top, low = pl.ds(0, SPLIT_ROWS), pl.ds(SPLIT_ROWS, 512 - SPLIT_ROWS)
        near, far, far_b = {}, {}, {}
        for d in (2, 1, 3, 0):
            ready(d, 1)
            far_b[d] = net.put(src.at[at(d, 1), low], rb_buf.at[d], across)
            if d:
                far[d] = net.put(src.at[at(d, 1), top], ra_buf.at[2 * d - 2], ring_peer[d])
        for d in (2, 1, 3, 0):
            ready(d, 0)
            if d:
                near[d] = net.put(src.at[at(d, 0), top], ra_buf.at[2 * d - 1], ring_peer[d])
        yield
        second = {}
        for d in (2, 1, 3):
            far_b[d].wait_recv()
            part = src[at(d, 0), low].astype(f32) + rb_buf[d].astype(f32)
            r2b_src[d - 1] = part.astype(bf16)
            second[d] = net.put(r2b_src.at[d - 1], r2b_buf.at[d - 1], ring_peer[d])
        part = src[at(0, 1), top].astype(f32)
        for d in (1, 3, 2):
            far[d].wait_recv()
            part += ra_buf[2 * d - 2].astype(f32)
        r2a_src[...] = part.astype(bf16)
        second_a = net.put(r2a_src, r2a_buf, across)
        yield
        part = src[at(0, 0), top].astype(f32)
        for d in (1, 3, 2):
            near[d].wait_recv()
            part += ra_buf[2 * d - 1].astype(f32)
        out[top, :] = part
        far_b[0].wait_recv()
        out[low, :] = src[at(0, 0), low].astype(f32) + rb_buf[0].astype(f32)
        yield
        second_a.wait_recv()
        out[top, :] += r2a_buf[...].astype(f32)
        part = out[low, :]
        for d in (1, 3, 2):
            second[d].wait_recv()
            part += r2b_buf[d - 1].astype(f32)
        out[low, :] = part
        yield

    def multiply(base, source, lanes, backward, unroll, begin, end):
        if begin == 0:
            acc[:, lanes] = jnp.zeros_like(acc[:, lanes])

        def body(step, carry):
            for u in range(unroll):
                p = step * unroll + u
                left = [tiles[meta[base, 2 * p + i]] for i in (0, 1)]
                right = [source[meta[base + 1, 2 * p + i]] for i in (0, 1)]
                right = jnp.concatenate(right, axis=0)
                if backward:
                    left = jnp.concatenate(left, axis=0)
                    form = (((0,), (0,)), ((), ()))
                else:
                    left = jnp.concatenate(left, axis=1)
                    form = (((1,), (0,)), ((), ()))
                product = lax.dot_general(left, right, form, preferred_element_type=f32)
                running = product + jnp.where(meta[base + 2, p] != 0, acc[:, lanes], 0.0)
                acc[:, lanes] = running
                prods[p, :, lanes] = running.astype(bf16)
            return carry

        lax.fori_loop(begin, end, body, 0)

    def count_some(begin, end):
        ones = jnp.ones((8, 256), bf16)

        def body(step, carry):
            for u in range(FWD_UNROLL):
                p = step * FWD_UNROLL + u
                pair = jnp.concatenate([tiles[meta[0, 2 * p + i]] for i in (0, 1)], axis=1)
                present = jnp.where(pair != 0, jnp.ones((), bf16), jnp.zeros((), bf16))
                found = lax.dot_general(
                    ones, present, (((1,), (1,)), ((), ())), preferred_element_type=f32
                )
                running = found + jnp.where(meta[2, p] != 0, degp[FWD_PAIRS], 0.0)
                degp[FWD_PAIRS] = running
                degp[p] = running
            return carry

        lax.fori_loop(begin, end, body, 0)

    def make_plan():
        count = count_ref[...]
        row_l, col_l = row_ref[...], col_ref[...]
        row_s, col_s = as_column(row_l), as_column(col_l)
        meta_v[0:4, :] = order_slots(row_l, row_s, col_s, count, ROW_BLOCKS, COL_BLOCKS, FWD_PAIRS)
        meta_v[4:8, :] = order_slots(col_l, col_s, row_s, count, COL_BLOCKS, ROW_BLOCKS, BWD_PAIRS)
        copy = pltpu.make_async_copy(meta_v, meta, local_sem.at[9])
        copy.start()
        tiles[SLOTS] = jnp.zeros((128, 128), bf16)
        prods[FWD_PAIRS] = jnp.zeros((128, 256), bf16)
        degp[FWD_PAIRS] = jnp.zeros((8, 128), f32)
        copy.wait()

    degree_copies = []

    def count_last():
        degp[FWD_PAIRS] = jnp.zeros((8, 128), f32)
        sub = lax.broadcasted_iota(i32, (8, 128), 0)
        for g in range(8):
            rows = jnp.zeros((8, 128), f32)
            for j in range(4):
                rows = jnp.where(sub == j, degp[meta[3, 4 * g + j]], rows)
            degs[g] = rows
        for d in range(4):
            for e in (0, 1):
                if (d, e) == (0, 0):
                    continue
                target = h_peer if d == 0 else (diagonal[d] if e else x_peer[d])
                index = ((x + d) % 4) * 2 + ((1 - h) if e else h)
                degree_copies.append(net.put(degs.at[index], degr.at[2 * d + e], target))
        for copy in loads[3:]:
            copy.wait()
        for j in range(4):
            own = jnp.concatenate([xg[f][4 * gr + j] for f in (0, 1)], axis=1)
            own_part[pl.ds(128 * j, 128), :] = (
                jnp.dot(own, w_self[...], preferred_element_type=f32) + bias_ref[...]
            )

    def feature_gather(f):
        def to_sibling(d, other):
            at = 4 * ((1 - a if other else a) * 8 + ((z + d) % 4) * 2 + core)
            shard = xg[f].at[pl.ds(at, 4)]
            return net.put(shard, shard, sib)

        return gather(
            xg[f],
            lambda ring, side: 4 * (side * 8 + ring * 2 + core),
            z,
            a,
            z_peer,
            a_peer,
            to_sibling,
        )

    def rows_at(d, other):
        return ((x + d) % 4) * 2 + ((1 - h) if other else h)

    def row_scatter(f):
        def rows_ready(d, other):
            shard = rows_at(d, other)
            for j in range(4):
                rowsum[f, shard, pl.ds(128 * j, 128), :] = prods[
                    meta[3, 4 * shard + j], :, pl.ds(128 * f, 128)
                ]

        bufs = [buf.at[f] for buf in fwd_bufs]
        return scatter(
            bufs, rowsum.at[f], total.at[f], rows_at, x, h, x_peer, h_peer, rows_ready
        )

    def forward_part(f, begin, end):
        multiply(0, xg[f], pl.ds(128 * f, 128), False, FWD_UNROLL, begin, end)

    get = [feature_gather(0), feature_gather(1)]
    put = [row_scatter(0), row_scatter(1)]
    next(get[0])
    make_plan()
    loads[2].wait()
    next(get[0])
    count_some(0, 2)
    next(get[0])
    next(get[1])
    count_some(2, 6)
    next(get[0])
    count_some(6, 8)
    count_last()
    next(get[0])
    forward_part(0, 0, 2)
    next(get[1])
    forward_part(0, 2, 4)
    next(get[1])
    forward_part(0, 4, 6)
    next(get[1])
    forward_part(0, 6, 8)
    next(put[0])
    next(get[1])
    forward_part(1, 0, 8)
    next(put[0])
    next(put[1])
    next(put[0])
    next(put[1])
    next(put[0])
    next(put[1])
    next(put[1])

    degree = degs[gc]
    for copy in degree_copies:
        copy.wait_recv()
    for slot in range(1, 8):
        degree += degr[slot]
    degree = jnp.maximum(degree, 1.0)
    def dense_block(j):
        rows = pl.ds(128 * j, 128)
        counts = jnp.broadcast_to(degree[j : j + 1, :], (128, 128)).T
        counts = jnp.concatenate([counts, counts], axis=1)
        summed = jnp.concatenate([total[f, rows, :] for f in (0, 1)], axis=1)
        mean = (summed / counts).astype(bf16)
        neigh[rows, :] = mean
        preact = own_part[rows, :] + jnp.dot(mean, w_neigh[...], preferred_element_type=f32)
        sigma = jax.nn.sigmoid(preact)
        act_v[rows, :] = (preact * sigma).astype(bf16)
        grad = cot[rows, :].astype(f32) * sigma * (1.0 + preact * (1.0 - sigma))
        grad = grad.astype(bf16)
        grad_pre[rows, :] = grad
        projected = lax.dot_general(
            grad, w_neigh[...], (((1,), (1,)), ((), ())), preferred_element_type=f32
        )
        bg[4 * gc + j] = (projected / counts).astype(bf16)


    contract_rows = (((0,), (0,)), ((), ()))
    state = {}

    def weight_grads():
        grad = grad_pre[...]
        for f in (0, 1):
            own = jnp.concatenate([xg[f][4 * gr + j] for j in range(4)], axis=0)
            wg[0, pl.ds(128 * f, 128), :] = lax.dot_general(
                own, grad, contract_rows, preferred_element_type=f32
            )
        wg[1, 0:256, :] = lax.dot_general(
            neigh[...], grad, contract_rows, preferred_element_type=f32
        )
        bias = jnp.sum(grad.astype(f32), axis=0, keepdims=True)
        for side in (0, 1):
            wg[side, 256:264, :] = jnp.broadcast_to(bias, (8, 256))
        state["s"] = [net.put(wg.at[1 - core], rs_, sib)]
        own_part[...] = lax.dot_general(
            grad, w_self[...], (((1,), (1,)), ((), ())), preferred_element_type=f32
        )

    def sum_sib():
        for copy in state["s"]:
            copy.wait_recv()
        both = wg[core] + rs_[...]
        for g in range(8):
            w1[g, 0:32, :] = both[32 * g : 32 * g + 32, :]
            w1[g, 32:40, :] = both[256:264, :]
        rx_[gc] = w1[gc]
        state["x"] = [net.put(w1.at[to], rx_.at[gc], target) for to, target in row_peers]

    def sum_row():
        for copy in state["x"]:
            copy.wait_recv()
        part = rx_[0]
        for g in range(1, 8):
            part += rx_[g]
        w2[...] = part
        rz_[z * 2 + a] = part
        state["z"] = [net.put(w2, rz_.at[z * 2 + a], target) for target in col_peers]

    def sum_all():
        for copy in state["z"]:
            copy.wait_recv()
        part = rz_[0]
        for g in range(1, 8):
            part += rz_[g]
        mine = pl.ds(core * 256 + gc * 32, 32)
        wfull[mine, :] = part[0:32, :] * (1.0 / 256.0)
        gbias_out[...] = part[32:33, :] * (1.0 / 256.0)
        piece = wfull.at[mine]
        state["gx"] = [net.put(piece, piece, target) for _, target in row_peers]

    def share_sib():
        for copy in state["gx"]:
            copy.wait_recv()
        half = wfull.at[pl.ds(core * 256, 256)]
        state["gs"] = [net.put(half, half, sib)]

    def no_forward(d, other):
        return None

    def cols_at(d, other):
        return ((z + d) % 4) * 2 + ((1 - a) if other else a)

    def block_of(d, other, core_):
        return 4 * (((1 - a) if other else a) * 8 + ((z + d) % 4) * 2 + core_)

    to_sib = {}

    def cols_to_sibling():
        for other in (1, 0):
            for d in (2, 1, 3, 0):
                shard = cols_at(d, other)
                for j in range(4):
                    csend[shard, pl.ds(128 * j, 128), :] = prods[
                        meta[7, block_of(d, other, 1 - core) + j]
                    ]
                to_sib[d, other] = net.put(csend.at[shard], crecv.at[shard], sib)

    def cols_ready(d, other):
        shard = cols_at(d, other)
        to_sib[d, other].wait_recv()
        for j in range(4):
            rows = pl.ds(128 * j, 128)
            mine = prods[meta[7, block_of(d, other, core) + j]].astype(f32)
            csum[shard, rows, :] = (mine + crecv[shard, rows, :].astype(f32)).astype(bf16)

    def weights_out():
        for copy in state["gs"]:
            copy.wait_recv()
        stores.append(pltpu.make_async_copy(wfull, gweight_out, local_sem.at[7]))
        stores[1].start()

    get = gather(bg, lambda ring, side: 4 * (ring * 2 + side), x, h, x_peer, h_peer, no_forward, dense_block)
    put = scatter(bwd_bufs, csum, total_back, cols_at, z, a, z_peer, a_peer, cols_ready)
    every = pl.ds(0, 256)
    next(get)
    stores = [pltpu.make_async_copy(act_v, act_out, local_sem.at[6])]
    stores[0].start()
    next(get)
    next(get)
    weight_grads()
    next(get)
    next(get)
    sum_sib()
    prods[BWD_PAIRS] = jnp.zeros((128, 256), bf16)
    multiply(4, bg, every, True, BWD_UNROLL, 0, 4)
    sum_row()
    multiply(4, bg, every, True, BWD_UNROLL, 4, 8)
    cols_to_sibling()
    sum_all()
    next(put)
    next(put)
    share_sib()
    next(put)
    weights_out()
    next(put)
    gfeat_v[...] = (own_part[...] + total_back[...]).astype(bf16)
    stores.append(pltpu.make_async_copy(gfeat_v, gfeat_out, local_sem.at[8]))
    stores[2].start()
    net.finish()
    for copy in stores:
        copy.wait()


def layer(count, rows, cols, features, tiles, w_self, w_neigh, bias, cotangent):
    low = 512 - SPLIT_ROWS
    def scatter_bufs(*lead, width):
        return [
            VMEM((*lead, 6, SPLIT_ROWS, width), bf16),
            VMEM((*lead, 4, low, width), bf16),
            VMEM((*lead, SPLIT_ROWS, width), bf16),
            VMEM((*lead, SPLIT_ROWS, width), bf16),
            VMEM((*lead, 3, low, width), bf16),
            VMEM((*lead, 3, low, width), bf16),
        ]

    scratch = [
        VMEM((8, 512), i32),
        SMEM((8, 512), i32),
        VMEM((512, 256), bf16),
        VMEM((512, 256), bf16),
        VMEM((SLOTS + 1, 128, 128), bf16),
        [VMEM((COL_BLOCKS, 128, 128), bf16)] * 2,
        VMEM((BWD_PAIRS + 1, 128, 256), bf16),
        VMEM((128, 256), f32),
        VMEM((FWD_PAIRS + 1, 8, 128), f32),
        VMEM((8, 8, 128), f32),
        VMEM((8, 8, 128), f32),
        VMEM((2, 8, 512, 128), bf16),
        VMEM((ROW_BLOCKS, 128, 256), bf16),
        VMEM((8, 512, 256), bf16),
        VMEM((8, 512, 256), bf16),
        VMEM((8, 512, 256), bf16),
        scatter_bufs(2, width=128),
        scatter_bufs(width=256),
        VMEM((2, 512, 128), f32),
        VMEM((512, 256), f32),
        VMEM((512, 256), f32),
        VMEM((256, 256), bf16),
        VMEM((256, 256), bf16),
        VMEM((512, 256), bf16),
        VMEM((512, 256), bf16),
        VMEM((512, 256), bf16),
        VMEM((2, 264, 256), f32),
        VMEM((264, 256), f32),
        VMEM((8, 40, 256), f32),
        VMEM((8, 40, 256), f32),
        VMEM((40, 256), f32),
        VMEM((8, 40, 256), f32),
        VMEM((512, 256), f32),
        pltpu.SemaphoreType.DMA((SEMS,)),
        pltpu.SemaphoreType.DMA((SEMS,)),
        pltpu.SemaphoreType.DMA((10,)),
    ]
    anywhere = pl.BlockSpec(memory_space=pl.ANY)
    return pl.pallas_call(
        layer_kernel,
        out_shape=(
            jax.ShapeDtypeStruct((512, 256), bf16),
            jax.ShapeDtypeStruct((512, 256), bf16),
            jax.ShapeDtypeStruct((512, 256), f32),
            jax.ShapeDtypeStruct((1, 256), f32),
        ),
        in_specs=[pl.BlockSpec(memory_space=VMEM)] * 3
        + [anywhere] * 4
        + [pl.BlockSpec(memory_space=VMEM), anywhere],
        out_specs=[anywhere] * 3 + [pl.BlockSpec(memory_space=VMEM)],
        scratch_shapes=scratch,
        compiler_params=pltpu.CompilerParams(
            collective_id=0, has_side_effects=True, vmem_limit_bytes=60 * 1024 * 1024
        ),
        name="layer",
    )(count, rows, cols, features, tiles, w_self, w_neigh, bias, cotangent)


def hand_over_kernel(act, gfeat, gweight, gbias, act_out, gfeat_out, gself, gneigh, gbias_out):
    act_out[...] = act[...]
    gfeat_out[...] = gfeat[...]
    gself[...] = gweight[0:256, :]
    gneigh[...] = gweight[256:512, :]
    gbias_out[...] = gbias[0, :]


def hand_over(act, gfeat, gweight, gbias):
    whole = pl.BlockSpec(memory_space=VMEM)
    return pl.pallas_call(
        hand_over_kernel,
        out_shape=(
            jax.ShapeDtypeStruct((512, 256), bf16),
            jax.ShapeDtypeStruct((512, 256), bf16),
            jax.ShapeDtypeStruct((256, 256), f32),
            jax.ShapeDtypeStruct((256, 256), f32),
            jax.ShapeDtypeStruct((256,), f32),
        ),
        in_specs=[whole] * 4,
        out_specs=[whole] * 5,
        compiler_params=pltpu.CompilerParams(vmem_limit_bytes=60 * 1024 * 1024),
        name="hand_over",
    )(act, gfeat, gweight, gbias)


def local(
    features,
    block_values,
    block_row,
    block_col,
    block_count,
    weight_self,
    weight_neigh,
    bias,
    cotangent,
):
    results = layer(
        block_count,
        block_row.reshape(1, SLOTS),
        block_col.reshape(1, SLOTS),
        features.reshape(4, 128, 256),
        block_values.reshape(SLOTS, 128, 128),
        weight_self,
        weight_neigh,
        bias.reshape(1, 256),
        cotangent,
    )
    return hand_over(*results)


def solution(mesh):
    placed = (
        P(("gr", "gc"), None),
        P("gr", "gc", None, None, None),
        P("gr", "gc", None),
        P("gr", "gc", None),
        P("gr", "gc"),
        P(),
        P(),
        P(),
        P(("gr", "gc"), None),
    )
    return jax.shard_map(
        local,
        mesh=mesh,
        in_specs=placed,
        out_specs=(P(("gr", "gc"), None), P(("gr", "gc"), None), P(), P(), P()),
        check_vma=False,
    )
```
